256 devices in a mesh: row: 32 (over y, z_hi, x), col: 8 (over z_lo, core).
Axes of the slice: x: 4, y: 4, z: 8 (z_hi: 2, z_lo: 4; z = z_hi * 4 + z_lo), core: 2. Of those that a mesh axis runs over, the one named last changes fastest.
Arguments:
- pair: float32 [576, 576, 128], P('row', 'col'), may hold values from -6 to 6
- cotangent: float32 [576, 576, 128], P('row', 'col'), may hold values from -6 to 6
- residue_mask: int32 [576], replicated, may hold values 0 or 1
- ln_gain: float32 [128], replicated, may hold values from 0.25 to 1.75
- ln_bias: float32 [128], replicated, may hold values from -3 to 3
- proj_weight: float32 [128, 640], replicated, may hold values from -0.5 to 0.5
- proj_bias: float32 [640], replicated, may hold values from -3 to 3
- norm_gain: float32 [128], replicated, may hold values from 0.25 to 1.75
- norm_bias: float32 [128], replicated, may hold values from -3 to 3
- out_weight: float32 [128, 128], replicated, may hold values from -0.5 to 0.5
- out_bias: float32 [128], replicated, may hold values from -3 to 3
Outputs:
- update: float32 [576, 576, 128], P('row', 'col')
- grad_pair: float32 [576, 576, 128], P('row', 'col')
- grad_proj: float32 [128, 640], replicated
- grad_out: float32 [128, 128], replicated
The draws below stay inside these ranges and needn't reach their ends.
All inputs are finite; a program needn't handle non-finite values.
Results may differ from the reference program's by a relative error of at most 0.015.
Values may be sent and summed in bfloat16 or wider, within the bound.
No kernel may reach another device: no remote copies, remote signals or barrier semaphores. Data moves between devices by JAX's collectives and lax.ppermute only.
A program may use at most 192 MiB of HBM per device.

```python
import jax
import jax.numpy as jnp
from jax import lax

C = 128
CH = 128
RD = 18
N = 576


def plant(values, own_key, low, top_value):
    longest = values.shape.index(max(values.shape))
    spots = []
    for shift in (0, 1):
        where = [jax.random.randint(jax.random.fold_in(own_key, axis), (), 0, length) for axis, length in enumerate(values.shape)]
        where[longest] = (where[longest] + shift) % values.shape[longest]
        spots.append(tuple(where))
    return values.at[spots[0]].set(low).at[spots[1]].set(top_value)


def raised(drawn, own_key, source, target, blocks, factor):
    def block_of(position):
        return (jnp.arange(drawn.shape[position]) // (drawn.shape[position] // blocks)).reshape((-1,) + (1,) * (drawn.ndim - 1 - position))

    near = jax.random.permutation(own_key, blocks)[block_of(target)]
    far = (block_of(target) + blocks // 2) % blocks
    return jnp.where((block_of(source) == near) | (block_of(source) == far), factor * drawn, drawn)


def level_of(rng, dims, cuts, smallest, top_value):
    def one(dim, shards_of):
        steps = jax.random.uniform(jax.random.fold_in(jax.random.fold_in(rng, 6), dim), (shards_of,), jnp.float32, smallest / len(cuts), top_value / len(cuts))
        return jnp.repeat(jnp.exp(steps), dims[dim] // shards_of).reshape((-1,) + (1,) * (len(dims) - dim - 1))

    level = one(*cuts[0])
    for cut in cuts[1:]:
        level = level * one(*cut)
    return level


def noise(key, shape, scale, limit, cuts=(), kind=jnp.bfloat16):
    factor_of = level_of(key, shape, cuts, -0.22, 0.18) if cuts else 1.0
    array = jax.random.normal(key, shape, jnp.float32) * scale * factor_of
    return jnp.minimum(jnp.maximum(array, -limit), limit).astype(kind)


def noise_with(rng, extent, deviation, reach, shards, heavy, kind=jnp.bfloat16):
    array = deviation * jax.random.normal(rng, extent, jnp.float32)
    if shards:
        array = array * level_of(rng, extent, shards, -0.22, 0.18)
    return jnp.clip(raised(array, jax.random.fold_in(rng, 3), *heavy), -reach, reach).astype(kind)


def setup_inputs(seed: int = 0) -> dict:
    key_list = jax.random.split(jax.random.key(seed), 12)
    pair = noise(key_list[0], (N, N, C), 1.0, 6.0, ((0, 32), (1, 8)), jnp.float32)
    cotangent = noise_with(key_list[1], (N, N, C), 1.0, 6.0, ((0, 32), (1, 8)), (0, 1, 32, 2.75), jnp.float32)
    residue_mask = plant((jax.random.randint(key_list[2], (N,), 0, 8) < 7).astype(jnp.int32), jax.random.fold_in(key_list[2], 1), 0, 1)
    ln_gain = jnp.clip(1.0 + 0.15 * jax.random.normal(key_list[3], (C,), jnp.float32), 0.25, 1.75)
    ln_bias = noise(key_list[4], (C,), 0.5, 3.0, (), jnp.float32)
    proj_weight = noise(key_list[5], (C, 4 * CH + C), C ** -0.5, 0.5, (), jnp.float32)
    proj_bias = noise(key_list[6], (4 * CH + C,), 0.5, 3.0, (), jnp.float32)
    norm_gain = jnp.clip(1.0 + 0.15 * jax.random.normal(key_list[7], (CH,), jnp.float32), 0.25, 1.75)
    norm_bias = noise(key_list[8], (CH,), 0.5, 3.0, (), jnp.float32)
    out_weight = noise(key_list[9], (CH, C), CH ** -0.5, 0.5, (), jnp.float32)
    out_bias = noise(key_list[10], (C,), 0.5, 3.0, (), jnp.float32)
    return dict(pair=pair, cotangent=cotangent, residue_mask=residue_mask, ln_gain=ln_gain, ln_bias=ln_bias, proj_weight=proj_weight, proj_bias=proj_bias, norm_gain=norm_gain, norm_bias=norm_bias, out_weight=out_weight, out_bias=out_bias)


def layer_norm(values, gain, bias):
    centred = values - lax.optimization_barrier(jnp.mean(values, axis=-1, keepdims=True))
    spread = lax.optimization_barrier(jnp.mean(centred * centred, axis=-1, keepdims=True))
    return centred * lax.rsqrt(spread + 1e-05) * gain + bias

def project(pair, mask2d, ln_gain, ln_bias, proj_weight, proj_bias):
    normed = layer_norm(pair, ln_gain, ln_bias)
    hidden = jnp.einsum('abc,cd->abd', normed, proj_weight, precision=lax.Precision.HIGHEST) + proj_bias
    width = (proj_weight.shape[1] - pair.shape[-1]) // 4
    masked = mask2d[:, :, None]
    left = masked * jax.nn.sigmoid(hidden[:, :, width:2 * width]) * hidden[:, :, :width]
    right = masked * jax.nn.sigmoid(hidden[:, :, 3 * width:4 * width]) * hidden[:, :, 2 * width:3 * width]
    return (left, right, hidden[:, :, 4 * width:])

def finish(mixed, gate_logit, norm_gain, norm_bias, out_weight, out_bias):
    normed = layer_norm(mixed, norm_gain, norm_bias)
    result = jnp.einsum('abc,cd->abd', normed, out_weight, precision=lax.Precision.HIGHEST) + out_bias
    return jax.nn.sigmoid(gate_logit) * result

def reference(pair, cotangent, residue_mask, ln_gain, ln_bias, proj_weight, proj_bias, norm_gain, norm_bias, out_weight, out_bias):
    valid = residue_mask.astype(jnp.float32)
    mask2d = valid[:, None] * valid[None, :]
    (left, right, gate_logit), pull_in = jax.vjp(lambda p, w: project(p, mask2d, ln_gain, ln_bias, w, proj_bias), pair, proj_weight)
    left_b = lax.optimization_barrier(left.astype(jnp.bfloat16)).astype(jnp.float32)
    right_b = lax.optimization_barrier(right.astype(jnp.bfloat16)).astype(jnp.float32)
    mixed = jnp.einsum('ikc,jkc->ijc', left_b, right_b, precision=lax.Precision.HIGHEST)
    update, pull_out = jax.vjp(lambda x, g, w: finish(x, g, norm_gain, norm_bias, w, out_bias), mixed, gate_logit, out_weight)
    d_mixed, d_gate, grad_out = pull_out(cotangent)
    d_mixed_b = lax.optimization_barrier(d_mixed.astype(jnp.bfloat16)).astype(jnp.float32)
    d_left = jnp.einsum('ijc,jkc->ikc', d_mixed_b, right_b, precision=lax.Precision.HIGHEST)
    width = d_mixed_b.shape[-1]
    total = d_mixed_b.shape[0]
    grouped_d = d_mixed_b.reshape(total // RD, RD, total, width)
    grouped_left = left_b.reshape(total // RD, RD, total, width)

    def add_group(carry, pieces):
        part = jnp.einsum('ijc,ikc->jkc', pieces[0], pieces[1], precision=lax.Precision.HIGHEST)
        rounded = lax.optimization_barrier(part.astype(jnp.bfloat16)).astype(jnp.float32)
        return (carry + rounded, None)
    d_right, _ = lax.scan(add_group, jnp.zeros((total, total, width), jnp.float32), (grouped_d, grouped_left))
    grad_pair, grad_proj = pull_in((d_left, d_right, d_gate))
    return (update, grad_pair, grad_proj, grad_out)
```

```python
import jax
import jax.numpy as jnp
from jax import lax
from jax.sharding import PartitionSpec as P

BOTH = ("row", "col")
SWAP = [(0, 1), (1, 0), (2, 3), (3, 2), (4, 5), (5, 4), (6, 7), (7, 6)]


def layer_norm(values, gain, bias):
    centred = values - jnp.mean(values, axis=0, keepdims=True)
    spread = jnp.mean(centred * centred, axis=0, keepdims=True)
    return centred * lax.rsqrt(spread + 1e-05) * gain[:, None] + bias[:, None]


def project(pair, mask, ln_gain, ln_bias, proj_weight, proj_bias):
    normed = layer_norm(pair, ln_gain, ln_bias)
    hidden = (
        jnp.einsum("cp,cd->dp", normed, proj_weight, precision=lax.Precision.HIGHEST)
        + proj_bias[:, None]
    )
    width = (proj_weight.shape[1] - pair.shape[0]) // 4
    left = mask * jax.nn.sigmoid(hidden[width : 2 * width]) * hidden[:width]
    right = mask * jax.nn.sigmoid(hidden[3 * width : 4 * width]) * hidden[2 * width : 3 * width]
    return (left, right, hidden[4 * width :])


def finish(mixed, gate_logit, norm_gain, norm_bias, out_weight, out_bias):
    normed = layer_norm(mixed, norm_gain, norm_bias)
    result = (
        jnp.einsum("cp,cd->dp", normed, out_weight, precision=lax.Precision.HIGHEST)
        + out_bias[:, None]
    )
    return jax.nn.sigmoid(gate_logit) * result


def exchange(chunks):
    return lax.all_to_all(chunks, BOTH, 0, 0, tiled=True)


def shards(
    pair,
    cotangent,
    residue_mask,
    ln_gain,
    ln_bias,
    proj_weight,
    proj_bias,
    norm_gain,
    norm_bias,
    out_weight,
    out_bias,
):
    rows, cols, width = pair.shape
    row_n, col_n = 32, 8
    devices = row_n * col_n
    half = rows // 2
    places = rows * cols
    piece = half * cols
    total = row_n * rows
    core = lax.axis_index("col") % 2
    row_start = lax.axis_index("row") * rows
    col_start = lax.axis_index("col") * cols
    valid = residue_mask.astype(jnp.float32)
    row_valid = lax.dynamic_slice_in_dim(valid, row_start, rows)
    col_valid = lax.dynamic_slice_in_dim(valid, col_start, cols)
    mask = (row_valid[:, None] * col_valid[None, :]).reshape(1, places)
    (left, right, gate_logit), pull_in = jax.vjp(
        lambda p, w: project(p, mask, ln_gain, ln_bias, w, proj_bias),
        pair.reshape(places, width).T,
        proj_weight,
    )
    chunks = jnp.stack(
        [
            left.astype(jnp.bfloat16).reshape(devices, piece),
            right.astype(jnp.bfloat16).reshape(devices, piece),
        ],
        axis=1,
    )
    got = exchange(chunks).reshape(row_n, col_n, 2, half, cols)
    got = got.transpose(2, 0, 3, 1, 4).reshape(2, row_n * half, total)
    left_h, right_h = got[0], got[1]
    right_o = lax.ppermute(right_h, "col", SWAP)
    first = core == 0
    right_all = jnp.concatenate(
        [jnp.where(first, right_h, right_o), jnp.where(first, right_o, right_h)], axis=0
    )
    mixed = jnp.einsum("ik,jk->ij", left_h, right_all, preferred_element_type=jnp.float32)
    group = row_n // col_n
    mixed = mixed.astype(jnp.bfloat16).reshape(row_n, half, 2, col_n, group, half)
    mixed = mixed.transpose(0, 3, 1, 4, 2, 5).reshape(devices, piece)
    mixed = exchange(mixed).reshape(width, places).astype(jnp.float32)
    update, pull_out = jax.vjp(
        lambda x, g, w: finish(x, g, norm_gain, norm_bias, w, out_bias),
        mixed,
        gate_logit,
        out_weight,
    )
    d_mixed, d_gate, grad_out = pull_out(cotangent.reshape(places, width).T)
    d_mixed = exchange(d_mixed.astype(jnp.bfloat16).reshape(devices, piece))
    d_mixed = d_mixed.reshape(row_n, col_n, half, group, 2, half)
    d_mixed = d_mixed.transpose(0, 2, 4, 1, 3, 5).reshape(row_n * half, total)
    d_left = jnp.einsum("ij,jk->ik", d_mixed, right_all, preferred_element_type=jnp.float32)
    terms = jnp.einsum("ij,ik->jk", d_mixed, left_h, preferred_element_type=jnp.float32)
    low, high = terms[: total // 2], terms[total // 2 :]
    away = jnp.where(first, high, low).astype(jnp.bfloat16)
    d_right = jnp.where(first, low, high) + lax.ppermute(away, "col", SWAP).astype(jnp.float32)
    back = jnp.stack([d_left.astype(jnp.bfloat16), d_right.astype(jnp.bfloat16)], axis=0)
    back = back.reshape(2, row_n, half, col_n, cols).transpose(1, 3, 0, 2, 4)
    back = exchange(back.reshape(devices, 2, piece)).astype(jnp.float32)
    back = back.reshape(width, 2, 2, piece).transpose(2, 0, 1, 3).reshape(2, width, places)
    grad_pair, proj_term = pull_in((back[0], back[1], d_gate))
    grads = jnp.concatenate([proj_term, grad_out], axis=1)
    pieces = exchange(grads.reshape(devices, -1))
    summed = jnp.sum(pieces, axis=0, keepdims=True)
    grads = exchange(jnp.broadcast_to(summed, pieces.shape)).reshape(grads.shape)
    shape = (rows, cols, width)
    return (
        update.T.reshape(shape),
        grad_pair.T.reshape(shape),
        grads[:, : proj_term.shape[1]],
        grads[:, proj_term.shape[1] :],
    )


def solution(mesh):
    in_specs = (P("row", "col", None), P("row", "col", None)) + (P(),) * 9
    out_specs = (P("row", "col", None), P("row", "col", None), P(), P())
    return jax.shard_map(shards, mesh=mesh, in_specs=in_specs, out_specs=out_specs, check_vma=False)
```

```python
import functools

import jax
import jax.numpy as jnp
import numpy as np
from jax import lax
from jax.experimental import pallas as pl
from jax.experimental.pallas import tpu as pltpu
from jax.sharding import PartitionSpec as P

BOTH = ("row", "col")
SWAP = [(0, 1), (1, 0), (2, 3), (3, 2), (4, 5), (5, 4), (6, 7), (7, 6)]
ROWS, COLS, WIDTH = 18, 72, 128
ROW_N, COL_N = 32, 8
DEVICES = ROW_N * COL_N
HALF = ROWS // 2
PIECE = HALF * COLS
WIRE = 768
LANES = 2 * WIRE
TOTAL = ROW_N * ROWS
GROUP = ROW_N // COL_N
STEP = 256
F32, BF16 = jnp.float32, jnp.bfloat16
EXACT = lax.Precision.HIGHEST


def one_hot(targets, length):
    table = np.zeros((len(targets), length), np.float32)
    table[np.arange(len(targets)), targets] = 1
    return jnp.asarray(table, BF16)


def tables():
    col, row = np.divmod(np.arange(DEVICES), ROW_N)
    by_col = one_hot(row * COL_N + col, DEVICES)
    row, col = np.divmod(np.arange(DEVICES), COL_N)
    by_row = one_hot(col * ROW_N + row, DEVICES)
    half, channel = np.divmod(np.arange(DEVICES), WIDTH)
    by_half = one_hot(channel * 2 + half, DEVICES)
    channel, half = np.divmod(np.arange(DEVICES), 2)
    by_channel = one_hot(half * WIDTH + channel, DEVICES)
    place, row = np.divmod(np.arange(TOTAL), ROW_N)
    col, part = np.divmod(row, GROUP)
    spread = one_hot(col * 128 + part * ROWS + place, COL_N * 128)
    return by_col, by_row, by_half, by_channel, spread


def dot(a, b, contract=((1,), (0,)), precision=None):
    return lax.dot_general(
        a, b, (contract, ((), ())), precision=precision, preferred_element_type=F32
    )


def move(table, values):
    return dot(table[...], values).astype(BF16)


def sigmoid(x):
    return 0.5 * jnp.tanh(0.5 * x) + 0.5


def normalise(values):
    centred = values - jnp.mean(values, axis=0, keepdims=True)
    spread = jnp.mean(centred * centred, axis=0, keepdims=True)
    scale = lax.rsqrt(spread + 1e-05)
    return centred * scale, scale


def normalise_back(d_hat, hat, scale):
    return scale * (
        d_hat
        - jnp.mean(d_hat, axis=0, keepdims=True)
        - hat * jnp.mean(d_hat * hat, axis=0, keepdims=True)
    )


def fill(padded, block):
    for half in range(2):
        padded[pl.ds(half * WIRE, PIECE), :] = block[pl.ds(half * PIECE, PIECE), :]
        padded[pl.ds(half * WIRE + PIECE, WIRE - PIECE), :] = jnp.zeros(
            (WIRE - PIECE, WIDTH), F32
        )


def drain(block, padded):
    for half in range(2):
        block[pl.ds(half * PIECE, PIECE), :] = padded[pl.ds(half * WIRE, PIECE), :]


def place_of(step):
    per = WIRE // STEP
    half = step // per
    return (
        pl.ds(pl.multiple_of(half * WIDTH, WIDTH), WIDTH),
        pl.ds(pl.multiple_of((step - half * per) * STEP, STEP), STEP),
    )


def lanes_of(step):
    return pl.ds(pl.multiple_of(step * STEP, STEP), STEP)


def project_kernel(
    pair, weight_t, bias, gain, shift, mask, by_channel, wire, gate, padded, left_s, right_s
):
    fill(padded, pair)

    @pl.loop(0, LANES // STEP)
    def _(step):
        lanes = lanes_of(step)
        hat, _ = normalise(padded[lanes, :].T)
        normed = hat * gain[...] + shift[...]
        hidden = dot(weight_t[...], normed, precision=EXACT) + bias[...]
        valid = mask[:, lanes]
        rows, cols = place_of(step)
        left = valid * sigmoid(hidden[WIDTH : 2 * WIDTH]) * hidden[:WIDTH]
        left_s[rows, cols] = left.astype(BF16)
        right = valid * sigmoid(hidden[3 * WIDTH : 4 * WIDTH]) * hidden[2 * WIDTH : 3 * WIDTH]
        right_s[rows, cols] = right.astype(BF16)
        gate[:, lanes] = hidden[4 * WIDTH :]

    wire[:, :WIRE] = move(by_channel, left_s[...])
    wire[:, WIRE:] = move(by_channel, right_s[...])


def unpack(values, out, base):
    keep = lax.broadcasted_iota(jnp.int32, (DEVICES, 128), 1) < COLS
    for i in range(HALF):
        tile, offset = divmod(i * COLS, 128)
        part = values[:, tile * 128 : tile * 128 + 256]
        if offset:
            part = pltpu.roll(part, 256 - offset, 1)
        part = jnp.where(keep, part[:, :128], 0.0).astype(BF16)
        for q in range(COL_N):
            out[pl.ds(base + i * ROW_N, ROW_N), q * 128 : (q + 1) * 128] = part[
                q * ROW_N : (q + 1) * ROW_N
            ]


def pack(values, out):
    out[...] = jnp.zeros_like(out)
    for i in range(HALF):
        tile, offset = divmod(i * COLS, 128)
        part = jnp.concatenate(
            [
                values[i * ROW_N : (i + 1) * ROW_N, q * 128 : (q + 1) * 128]
                for q in range(COL_N)
            ],
            axis=0,
        )
        part = jnp.concatenate([part, jnp.zeros_like(part)], axis=1)
        if offset:
            part = pltpu.roll(part, offset, 1)
        out[:, tile * 128 : tile * 128 + 256] += part


def mix_kernel(
    core, left_w, right_w, other_w, by_col, by_row, spread, wire, left_m, right_m, packed
):
    own = core[0] * (TOTAL // 2)
    away = (TOTAL // 2) - own
    unpack(dot(by_col[...], left_w[...]), left_m, 0)
    unpack(dot(by_col[...], right_w[...]), right_m, pl.multiple_of(own, 32))
    unpack(dot(by_col[...], other_w[...]), right_m, pl.multiple_of(away, 32))
    mixed = dot(left_m[...], right_m[...], ((1,), (1,))).astype(BF16)
    pack(dot(mixed, spread[...]), packed)
    wire[...] = move(by_row, packed[...].astype(BF16))


def finish_kernel(
    mixed_w, cotangent, gate, gain, shift, weight, weight_t, bias, by_half, by_channel,
    update, d_wire, d_gate, grad_out, mixed_s, padded, padded_out, d_mixed_s,
):
    fill(padded, cotangent)
    mixed_s[...] = dot(by_half[...], mixed_w[...])
    grad_out[...] = jnp.zeros_like(grad_out)

    @pl.loop(0, LANES // STEP)
    def _(step):
        lanes = lanes_of(step)
        rows, cols = place_of(step)
        hat, scale = normalise(mixed_s[rows, cols])
        normed = hat * gain[...] + shift[...]
        result = dot(weight_t[...], normed, precision=EXACT) + bias[...]
        opened = sigmoid(gate[:, lanes])
        padded_out[lanes, :] = (opened * result).T
        given = padded[lanes, :].T
        d_result = given * opened
        d_gate[:, lanes] = given * result * (opened * (1.0 - opened))
        grad_out[...] += dot(normed, d_result, ((1,), (1,)), EXACT)
        d_hat = dot(weight[...], d_result, precision=EXACT) * gain[...]
        d_mixed_s[rows, cols] = normalise_back(d_hat, hat, scale).astype(BF16)

    drain(update, padded_out)
    d_wire[...] = move(by_channel, d_mixed_s[...])


def unmix_kernel(
    core, d_w, left_m, right_m, by_col, by_row, spread, left_wire, own_wire, away_wire,
    d_mixed_m, terms, packed,
):
    own = core[0] * (TOTAL // 2)
    away = (TOTAL // 2) - own
    unpack(dot(by_col[...], d_w[...]), d_mixed_m, 0)
    d_mixed = dot(d_mixed_m[...], spread[...], ((1,), (1,))).astype(BF16)
    terms[...] = dot(d_mixed, left_m[...], ((0,), (0,)))
    pack(terms[pl.ds(pl.multiple_of(away, 32), TOTAL // 2), :], packed)
    away_wire[...] = move(by_row, packed[...].astype(BF16))
    pack(terms[pl.ds(pl.multiple_of(own, 32), TOTAL // 2), :], packed)
    own_wire[...] = move(by_row, packed[...].astype(BF16))
    pack(dot(d_mixed, right_m[...]), packed)
    left_wire[...] = move(by_row, packed[...].astype(BF16))


def pull_kernel(
    pair, d_left_w, d_right_w, d_gate, weight, weight_t, bias, gain, shift, mask, by_half,
    grad_pair, grad_proj, padded, padded_out, d_left_s, d_right_s,
):
    fill(padded, pair)
    d_left_s[...] = dot(by_half[...], d_left_w[...])
    d_right_s[...] = dot(by_half[...], d_right_w[...])
    grad_proj[...] = jnp.zeros_like(grad_proj)

    @pl.loop(0, LANES // STEP)
    def _(step):
        lanes = lanes_of(step)
        rows, cols = place_of(step)
        hat, scale = normalise(padded[lanes, :].T)
        normed = hat * gain[...] + shift[...]
        hidden = dot(weight_t[: 4 * WIDTH, :], normed, precision=EXACT) + bias[: 4 * WIDTH, :]
        valid = mask[:, lanes]
        parts = []
        for i, ref in enumerate((d_left_s, d_right_s)):
            value = hidden[2 * i * WIDTH : (2 * i + 1) * WIDTH]
            opened = sigmoid(hidden[(2 * i + 1) * WIDTH : (2 * i + 2) * WIDTH])
            given = ref[rows, cols] * valid * opened
            parts += [given, given * value * (1.0 - opened)]
        d_hidden = jnp.concatenate(parts + [d_gate[:, lanes]], axis=0)
        grad_proj[...] += dot(normed, d_hidden, ((1,), (1,)), EXACT)
        d_hat = dot(weight[...], d_hidden, precision=EXACT) * gain[...]
        padded_out[lanes, :] = normalise_back(d_hat, hat, scale).T

    drain(grad_pair, padded_out)


def call(kernel, outs, scratch, *args, smem=0):
    vmem = pl.BlockSpec(memory_space=pltpu.VMEM)
    return pl.pallas_call(
        kernel,
        out_shape=[jax.ShapeDtypeStruct(*o) for o in outs],
        in_specs=[pl.BlockSpec(memory_space=pltpu.SMEM)] * smem + [vmem] * (len(args) - smem),
        out_specs=[vmem] * len(outs),
        scratch_shapes=[pltpu.VMEM(*s) for s in scratch],
        compiler_params=pltpu.CompilerParams(vmem_limit_bytes=48 * 2**20),
    )(*args)


def exchange(chunks):
    return lax.all_to_all(chunks, BOTH, 0, 0, tiled=True)


def shards(
    pair,
    cotangent,
    residue_mask,
    ln_gain,
    ln_bias,
    proj_weight,
    proj_bias,
    norm_gain,
    norm_bias,
    out_weight,
    out_bias,
):
    by_col, by_row, by_half, by_channel, spread = tables()
    shape = pair.shape
    places = ROWS * COLS
    core = (lax.axis_index("col") % 2).astype(jnp.int32).reshape(1)
    valid = residue_mask.astype(F32)
    row_valid = lax.dynamic_slice_in_dim(valid, lax.axis_index("row") * ROWS, ROWS)
    col_valid = lax.dynamic_slice_in_dim(valid, lax.axis_index("col") * COLS, COLS)
    mask = (row_valid[:, None] * col_valid[None, :]).reshape(2, PIECE)
    mask = jnp.pad(mask, ((0, 0), (0, WIRE - PIECE))).reshape(1, LANES)
    pair = pair.reshape(places, WIDTH)
    cotangent = cotangent.reshape(places, WIDTH)
    column = lambda v: v.reshape(-1, 1)
    weight_t = proj_weight.T
    whole = ((LANES, WIDTH), F32)
    halves = lambda kind: ((DEVICES, WIRE), kind)

    wire, gate = call(
        project_kernel,
        [((DEVICES, LANES), BF16), ((WIDTH, LANES), F32)],
        [whole, halves(BF16), halves(BF16)],
        pair, weight_t, column(proj_bias), column(ln_gain), column(ln_bias), mask, by_channel,
    )
    got = exchange(wire.reshape(DEVICES, 2, WIRE))
    right_w = got[:, 1]
    other_w = lax.ppermute(right_w, "col", SWAP)
    wire, left_m, right_m = call(
        mix_kernel,
        [halves(BF16), ((TOTAL // 2, COL_N * 128), BF16), ((TOTAL, COL_N * 128), BF16)],
        [halves(F32)],
        core, got[:, 0], right_w, other_w, by_col, by_row, spread,
        smem=1,
    )
    got = exchange(wire.reshape(DEVICES, 2, WIRE // 2)).reshape(DEVICES, WIRE)
    update, wire, d_gate, grad_out = call(
        finish_kernel,
        [((places, WIDTH), F32), halves(BF16), ((WIDTH, LANES), F32), ((WIDTH, WIDTH), F32)],
        [halves(F32), whole, whole, halves(BF16)],
        got, cotangent, gate, column(norm_gain), column(norm_bias), out_weight, out_weight.T,
        column(out_bias), by_half, by_channel,
    )
    got = exchange(wire.reshape(DEVICES, 2, WIRE // 2)).reshape(DEVICES, WIRE)
    left_wire, own_wire, away_wire = call(
        unmix_kernel,
        [halves(BF16)] * 3,
        [((TOTAL // 2, COL_N * 128), BF16), ((TOTAL, COL_N * 128), F32), halves(F32)],
        core, got, left_m, right_m, by_col, by_row, spread,
        smem=1,
    )
    other_wire = lax.ppermute(away_wire, "col", SWAP)
    right_wire = (own_wire.astype(F32) + other_wire.astype(F32)).astype(BF16)
    got = exchange(jnp.stack([left_wire, right_wire], axis=1))
    grad_pair, proj_term = call(
        pull_kernel,
        [((places, WIDTH), F32), ((WIDTH, 5 * WIDTH), F32)],
        [whole, whole, halves(F32), halves(F32)],
        pair, got[:, 0], got[:, 1], d_gate, proj_weight, weight_t, column(proj_bias),
        column(ln_gain), column(ln_bias), mask, by_half,
    )
    grads = jnp.concatenate([proj_term, grad_out], axis=1)
    pieces = exchange(grads.reshape(DEVICES, -1))
    summed = jnp.sum(pieces, axis=0, keepdims=True)
    grads = exchange(jnp.broadcast_to(summed, pieces.shape)).reshape(grads.shape)
    return (
        update.reshape(shape),
        grad_pair.reshape(shape),
        grads[:, : 5 * WIDTH],
        grads[:, 5 * WIDTH :],
    )


def solution(mesh):
    in_specs = (P("row", "col", None), P("row", "col", None)) + (P(),) * 9
    out_specs = (P("row", "col", None), P("row", "col", None), P(), P())
    return jax.shard_map(shards, mesh=mesh, in_specs=in_specs, out_specs=out_specs, check_vma=False)
```

```python
import jax
import jax.numpy as jnp
import numpy as np
from jax import lax
from jax.experimental import pallas as pl
from jax.experimental.pallas import tpu as pltpu
from jax.sharding import PartitionSpec as P

BOTH = ("row", "col")
SWAP = [(0, 1), (1, 0), (2, 3), (3, 2), (4, 5), (5, 4), (6, 7), (7, 6)]
ROWS, COLS, WIDTH = 18, 72, 128
ROW_N, COL_N = 32, 8
DEVICES = ROW_N * COL_N
HALF = ROWS // 2
PIECE = HALF * COLS
WIRE = 768
LANES = 2 * WIRE
TOTAL = ROW_N * ROWS
GROUP = ROW_N // COL_N
STEP = 256
F32, BF16 = jnp.float32, jnp.bfloat16


def one_hot(targets, length):
    table = np.zeros((len(targets), length), np.float32)
    table[np.arange(len(targets)), targets] = 1
    return jnp.asarray(table, BF16)


def tables():
    col, row = np.divmod(np.arange(DEVICES), ROW_N)
    by_col = one_hot(row * COL_N + col, DEVICES)
    row, col = np.divmod(np.arange(DEVICES), COL_N)
    by_row = one_hot(col * ROW_N + row, DEVICES)
    half, channel = np.divmod(np.arange(DEVICES), WIDTH)
    by_half = one_hot(channel * 2 + half, DEVICES)
    channel, half = np.divmod(np.arange(DEVICES), 2)
    by_channel = one_hot(half * WIDTH + channel, DEVICES)
    place, row = np.divmod(np.arange(TOTAL), ROW_N)
    col, part = np.divmod(row, GROUP)
    spread = one_hot(col * 128 + part * ROWS + place, COL_N * 128)
    return by_col, by_row, by_half, by_channel, spread


PLAIN = ((1,), (0,))
LAST = ((1,), (1,))


def dot(a, b, contract=PLAIN):
    return lax.dot_general(a, b, (contract, ((), ())), preferred_element_type=F32)


def split(x):
    high = x.astype(BF16)
    return high, (x - high.astype(F32)).astype(BF16)


def fine(a, b, contract=PLAIN):
    return dot(a[0], b[0], contract) + (dot(a[0], b[1], contract) + dot(a[1], b[0], contract))


def move(table, values):
    return dot(table[...], values).astype(BF16)


def sigmoid(x):
    return 0.5 * jnp.tanh(0.5 * x) + 0.5


def normalise(values):
    centred = values - jnp.mean(values, axis=0, keepdims=True)
    spread = jnp.mean(centred * centred, axis=0, keepdims=True)
    scale = lax.rsqrt(spread + 1e-05)
    return centred * scale, scale


def normalise_back(d_hat, hat, scale):
    return scale * (
        d_hat
        - jnp.mean(d_hat, axis=0, keepdims=True)
        - hat * jnp.mean(d_hat * hat, axis=0, keepdims=True)
    )


def column(ref):
    return jnp.broadcast_to(ref[...], (8, WIDTH)).T[:, :1]


def columns(ref):
    table = jnp.concatenate([ref[...], jnp.zeros((3, WIDTH), F32)], axis=0).T
    return [table[:, i : i + 1] for i in range(5)]


def fill(padded, block):
    for half in range(2):
        padded[pl.ds(half * WIRE, PIECE), :] = block[pl.ds(half * PIECE, PIECE), :]
        padded[pl.ds(half * WIRE + PIECE, WIRE - PIECE), :] = jnp.zeros(
            (WIRE - PIECE, WIDTH), F32
        )


def drain(block, padded):
    for half in range(2):
        block[pl.ds(half * PIECE, PIECE), :] = padded[pl.ds(half * WIRE, PIECE), :]


def place_of(step):
    per = WIRE // STEP
    half = step // per
    return (
        pl.ds(pl.multiple_of(half * WIDTH, WIDTH), WIDTH),
        pl.ds(pl.multiple_of((step - half * per) * STEP, STEP), STEP),
    )


def lanes_of(step):
    return pl.ds(pl.multiple_of(step * STEP, STEP), STEP)


def build_mask(place, valid_s, valid_v, mask):
    values = jnp.concatenate([valid_v[...].astype(F32), jnp.zeros((1, WIRE - TOTAL), F32)], axis=1)
    values = jnp.broadcast_to(values, (8, WIRE))
    shift = place[1] * COLS
    values = pltpu.roll(values, jnp.where(shift == 0, 0, WIRE - shift), 1)
    lane = lax.broadcasted_iota(jnp.int32, (8, WIRE), 1)
    values = jnp.where(lane < COLS, values, 0.0)
    shifted = [values] + [pltpu.roll(values, i * COLS, 1) for i in range(1, HALF)]
    for half in range(2):
        total = jnp.zeros((8, WIRE), F32)
        for i in range(HALF):
            row = valid_s[place[0] * ROWS + half * HALF + i].astype(F32)
            total = total + row * shifted[i]
        mask[:, half * WIRE : (half + 1) * WIRE] = total[:1]


def project_kernel(
    place, valid_s, valid_v, pair, weight, bias, gain, shift, by_channel,
    wire, mask,
    padded, left_s, right_s,
):
    build_mask(place, valid_s, valid_v, mask)
    fill(padded, pair)
    gain_c, shift_c = column(gain), column(shift)
    bias_c = jnp.concatenate(columns(bias)[:4], axis=0)
    weight_t = split(weight[:, : 4 * WIDTH].T)

    @pl.loop(0, LANES // STEP)
    def _(step):
        lanes = lanes_of(step)
        hat, _ = normalise(padded[lanes, :].T)
        hidden = fine(weight_t, split(hat * gain_c + shift_c)) + bias_c
        valid = mask[:, lanes]
        rows, cols = place_of(step)
        left = valid * sigmoid(hidden[WIDTH : 2 * WIDTH]) * hidden[:WIDTH]
        left_s[rows, cols] = left.astype(BF16)
        right = valid * sigmoid(hidden[3 * WIDTH : 4 * WIDTH]) * hidden[2 * WIDTH : 3 * WIDTH]
        right_s[rows, cols] = right.astype(BF16)

    wire[:, :WIRE] = move(by_channel, left_s[...])
    wire[:, WIRE:] = move(by_channel, right_s[...])


def prepare_kernel(
    mask, pair, cotangent, weight, bias, gain, shift, out_gain, out_weight,
    hat_o, scale_o, factors, opened_o, d_result_o, d_hat_o,
    padded, padded_c,
):
    fill(padded, pair)
    fill(padded_c, cotangent)
    gain_c, shift_c, out_gain_c = column(gain), column(shift), column(out_gain)
    bias_c = jnp.concatenate(columns(bias), axis=0)
    weight_t = split(weight[...].T)
    out_w = split(out_weight[...])

    @pl.loop(0, LANES // STEP)
    def _(step):
        lanes = lanes_of(step)
        hat, scale = normalise(padded[lanes, :].T)
        hat_o[:, lanes] = hat
        scale_o[:, lanes] = scale
        hidden = fine(weight_t, split(hat * gain_c + shift_c)) + bias_c
        valid = mask[:, lanes]
        for i in range(2):
            opened = sigmoid(hidden[(2 * i + 1) * WIDTH : (2 * i + 2) * WIDTH])
            factor = valid * opened
            factors[2 * i * WIDTH : (2 * i + 1) * WIDTH, lanes] = factor
            factors[(2 * i + 1) * WIDTH : (2 * i + 2) * WIDTH, lanes] = (
                factor * (1.0 - opened) * hidden[2 * i * WIDTH : (2 * i + 1) * WIDTH]
            )
        opened = sigmoid(hidden[4 * WIDTH :])
        opened_o[:, lanes] = opened
        d_result = padded_c[lanes, :].T * opened
        d_result_o[:, lanes] = d_result
        d_hat_o[:, lanes] = fine(out_w, split(d_result)) * out_gain_c


def unpack(values, out, base):
    keep = lax.broadcasted_iota(jnp.int32, (DEVICES, 128), 1) < COLS
    for i in range(HALF):
        tile, offset = divmod(i * COLS, 128)
        part = values[:, tile * 128 : tile * 128 + 256]
        if offset:
            part = pltpu.roll(part, 256 - offset, 1)
        part = jnp.where(keep, part[:, :128], 0.0).astype(BF16)
        for q in range(COL_N):
            out[pl.ds(base + i * ROW_N, ROW_N), q * 128 : (q + 1) * 128] = part[
                q * ROW_N : (q + 1) * ROW_N
            ]


def pack(values, out):
    out[...] = jnp.zeros_like(out)
    for i in range(HALF):
        tile, offset = divmod(i * COLS, 128)
        part = jnp.concatenate(
            [
                values[i * ROW_N : (i + 1) * ROW_N, q * 128 : (q + 1) * 128]
                for q in range(COL_N)
            ],
            axis=0,
        )
        part = jnp.concatenate([part, jnp.zeros_like(part)], axis=1)
        if offset:
            part = pltpu.roll(part, offset, 1)
        out[:, tile * 128 : tile * 128 + 256] += part


def mix_kernel(place, both_w, other_w, by_col, by_row, spread, wire, left_m, right_m, packed):
    own = place[2] * (TOTAL // 2)
    away = (TOTAL // 2) - own
    unpack(dot(by_col[...], both_w[:, :WIRE]), left_m, 0)
    unpack(dot(by_col[...], both_w[:, WIRE:]), right_m, pl.multiple_of(own, 32))
    unpack(dot(by_col[...], other_w[...]), right_m, pl.multiple_of(away, 32))
    mixed = dot(left_m[...], right_m[...], LAST).astype(BF16)
    pack(dot(mixed, spread[...]), packed)
    wire[...] = move(by_row, packed[...].astype(BF16))


def turn_kernel(mixed_w, d_hat, by_half, by_channel, wire, hat_o, mixed_s, d_mixed_s):
    mixed_s[...] = dot(by_half[...], mixed_w[...])

    @pl.loop(0, LANES // STEP)
    def _(step):
        lanes = lanes_of(step)
        rows, cols = place_of(step)
        hat, scale = normalise(mixed_s[rows, cols])
        hat_o[:, lanes] = hat
        d_mixed_s[rows, cols] = normalise_back(d_hat[:, lanes], hat, scale).astype(BF16)

    wire[...] = move(by_channel, d_mixed_s[...])


def update_kernel(
    hat_m, opened, d_result, hat, weight, gain, shift, out_gain, out_shift, out_weight, out_bias,
    update, grad_out, grad_gate, d_normed,
    padded,
):
    gain_c, shift_c = column(gain), column(shift)
    out_gain_c, out_shift_c, out_bias_c = column(out_gain), column(out_shift), column(out_bias)
    out_t = split(out_weight[...].T)
    gate_w = split(weight[:, 4 * WIDTH :])
    grad_out[...] = jnp.zeros_like(grad_out)
    grad_gate[...] = jnp.zeros_like(grad_gate)

    @pl.loop(0, LANES // STEP)
    def _(step):
        lanes = lanes_of(step)
        normed = split(hat_m[:, lanes] * out_gain_c + out_shift_c)
        result = fine(out_t, normed) + out_bias_c
        is_open = opened[:, lanes]
        padded[lanes, :] = (is_open * result).T
        given = d_result[:, lanes]
        grad_out[...] += fine(normed, split(given), LAST)
        d_gate = split(given * result * (1.0 - is_open))
        grad_gate[...] += fine(split(hat[:, lanes] * gain_c + shift_c), d_gate, LAST)
        d_normed[:, lanes] = fine(gate_w, d_gate)

    drain(update, padded)


def unmix_kernel(
    place, d_w, left_m, right_m, by_col, by_row, spread,
    left_wire, own_wire, away_wire,
    d_mixed_m, terms, packed,
):
    own = place[2] * (TOTAL // 2)
    away = (TOTAL // 2) - own
    unpack(dot(by_col[...], d_w[...]), d_mixed_m, 0)
    d_mixed = dot(d_mixed_m[...], spread[...], LAST).astype(BF16)
    terms[...] = dot(d_mixed, left_m[...], ((0,), (0,)))
    pack(terms[pl.ds(pl.multiple_of(away, 32), TOTAL // 2), :], packed)
    away_wire[...] = move(by_row, packed[...].astype(BF16))
    pack(terms[pl.ds(pl.multiple_of(own, 32), TOTAL // 2), :], packed)
    own_wire[...] = move(by_row, packed[...].astype(BF16))
    pack(dot(d_mixed, right_m[...]), packed)
    left_wire[...] = move(by_row, packed[...].astype(BF16))


def d_hidden_of(d_left_s, d_right_s, factors, step):
    rows, cols = place_of(step)
    lanes = lanes_of(step)
    parts = []
    for i, ref in enumerate((d_left_s, d_right_s)):
        given = ref[rows, cols]
        for j in range(2):
            start = (2 * i + j) * WIDTH
            parts.append(given * factors[start : start + WIDTH, lanes])
    return split(jnp.concatenate(parts, axis=0))


def weight_kernel(
    both_w, factors, hat, gain, shift, grad_gate, grad_out, by_half,
    grads,
    d_left_s, d_right_s, total,
):
    d_left_s[...] = dot(by_half[...], both_w[:, :WIRE])
    d_right_s[...] = dot(by_half[...], both_w[:, WIRE:])
    gain_c, shift_c = column(gain), column(shift)
    total[...] = jnp.zeros_like(total)

    @pl.loop(0, LANES // STEP)
    def _(step):
        d_hidden = d_hidden_of(d_left_s, d_right_s, factors, step)
        normed = split(hat[:, lanes_of(step)] * gain_c + shift_c)
        total[...] += fine(normed, d_hidden, LAST)

    grads[:WIDTH, :] = total[:, : 3 * WIDTH]
    grads[WIDTH:, :WIDTH] = total[:, 3 * WIDTH :]
    grads[WIDTH:, WIDTH : 2 * WIDTH] = grad_gate[...]
    grads[WIDTH:, 2 * WIDTH :] = grad_out[...]


def pair_kernel(
    both_w, factors, hat, scale, d_normed, weight, gain, by_half,
    grad_pair,
    d_left_s, d_right_s, padded,
):
    d_left_s[...] = dot(by_half[...], both_w[:, :WIRE])
    d_right_s[...] = dot(by_half[...], both_w[:, WIRE:])
    gain_c = column(gain)
    weight_s = split(weight[:, : 4 * WIDTH])

    @pl.loop(0, LANES // STEP)
    def _(step):
        lanes = lanes_of(step)
        d_hidden = d_hidden_of(d_left_s, d_right_s, factors, step)
        d_hat = (fine(weight_s, d_hidden) + d_normed[:, lanes]) * gain_c
        padded[lanes, :] = normalise_back(d_hat, hat[:, lanes], scale[:, lanes]).T

    drain(grad_pair, padded)


def call(kernel, outs, scratch, *args, smem=0, work=2e9):
    whole = lambda shape: pl.BlockSpec(shape, lambda i: (0,) * len(shape))
    scalars = [pl.BlockSpec(memory_space=pltpu.SMEM)] * smem
    return pl.pallas_call(
        kernel,
        grid=(1,),
        out_shape=[jax.ShapeDtypeStruct(*o) for o in outs],
        in_specs=scalars + [whole(a.shape) for a in args[smem:]],
        out_specs=[whole(o[0]) for o in outs],
        scratch_shapes=[pltpu.VMEM(*s) for s in scratch],
        compiler_params=pltpu.CompilerParams(vmem_limit_bytes=48 * 2**20),
        cost_estimate=pl.CostEstimate(flops=int(work), bytes_accessed=4 * 2**20, transcendentals=0),
    )(*args)


def exchange(chunks):
    return lax.all_to_all(chunks, BOTH, 0, 0, tiled=True)


def shards(
    pair,
    cotangent,
    residue_mask,
    ln_gain,
    ln_bias,
    proj_weight,
    proj_bias,
    norm_gain,
    norm_bias,
    out_weight,
    out_bias,
):
    by_col, by_row, by_half, by_channel, spread = tables()
    shape = pair.shape
    places = ROWS * COLS
    row, col = lax.axis_index("row"), lax.axis_index("col")
    place = jnp.stack([row, col, col % 2]).astype(jnp.int32)
    pair = pair.reshape(places, WIDTH)
    cotangent = cotangent.reshape(places, WIDTH)
    line = lambda v: v.reshape(-1, WIDTH)
    gain, shift, bias = line(ln_gain), line(ln_bias), line(proj_bias)
    out_gain, out_shift, out_bias = line(norm_gain), line(norm_bias), line(out_bias)
    whole = ((LANES, WIDTH), F32)
    turned = ((WIDTH, LANES), F32)
    square = ((WIDTH, WIDTH), F32)
    halves = lambda kind: ((DEVICES, WIRE), kind)

    wire, mask = call(
        project_kernel,
        [((DEVICES, LANES), BF16), ((1, LANES), F32)],
        [whole, halves(BF16), halves(BF16)],
        place, residue_mask, residue_mask.reshape(1, TOTAL), pair, proj_weight, bias, gain, shift,
        by_channel,
        smem=2,
    )
    got = exchange(wire.reshape(DEVICES, 2, WIRE)).reshape(DEVICES, LANES)
    hat, scale, factors, opened, d_result, d_hat = call(
        prepare_kernel,
        [turned, ((1, LANES), F32), ((4 * WIDTH, LANES), F32), turned, turned, turned],
        [whole, whole],
        mask, pair, cotangent, proj_weight, bias, gain, shift, out_gain, out_weight,
        work=1e10,
    )
    other_w = lax.ppermute(got[:, WIRE:], "col", SWAP)
    wire, left_m, right_m = call(
        mix_kernel,
        [halves(BF16), ((TOTAL // 2, COL_N * 128), BF16), ((TOTAL, COL_N * 128), BF16)],
        [halves(F32)],
        place, got, other_w, by_col, by_row, spread,
        smem=1,
    )
    got = exchange(wire.reshape(DEVICES, 2, WIRE // 2)).reshape(DEVICES, WIRE)
    wire, hat_m = call(
        turn_kernel,
        [halves(BF16), turned],
        [halves(F32), halves(BF16)],
        got, d_hat, by_half, by_channel,
    )
    got = exchange(wire.reshape(DEVICES, 2, WIRE // 2)).reshape(DEVICES, WIRE)
    update, grad_out, grad_gate, d_normed = call(
        update_kernel,
        [((places, WIDTH), F32), square, square, turned],
        [whole],
        hat_m, opened, d_result, hat, proj_weight, gain, shift, out_gain, out_shift, out_weight,
        out_bias,
        work=8e9,
    )
    left_wire, own_wire, away_wire = call(
        unmix_kernel,
        [halves(BF16)] * 3,
        [((TOTAL // 2, COL_N * 128), BF16), ((TOTAL, COL_N * 128), F32), halves(F32)],
        place, got, left_m, right_m, by_col, by_row, spread,
        smem=1,
    )
    other_wire = lax.ppermute(away_wire, "col", SWAP)
    right_wire = (own_wire.astype(F32) + other_wire.astype(F32)).astype(BF16)
    got = exchange(jnp.stack([left_wire, right_wire], axis=1)).reshape(DEVICES, LANES)
    (grads,) = call(
        weight_kernel,
        [((DEVICES, 3 * WIDTH), F32)],
        [halves(F32), halves(F32), ((WIDTH, 4 * WIDTH), F32)],
        got, factors, hat, gain, shift, grad_gate, grad_out, by_half,
    )
    pieces = exchange(grads)
    (grad_pair,) = call(
        pair_kernel,
        [((places, WIDTH), F32)],
        [halves(F32), halves(F32), whole],
        got, factors, hat, scale, d_normed, proj_weight, gain, by_half,
        work=8e9,
    )
    summed = jnp.sum(pieces, axis=0, keepdims=True)
    grads = exchange(jnp.broadcast_to(summed, pieces.shape))
    grad_proj = jnp.concatenate([grads[:WIDTH], grads[WIDTH:, : 2 * WIDTH]], axis=1)
    return update.reshape(shape), grad_pair.reshape(shape), grad_proj, grads[WIDTH:, 2 * WIDTH :]


def solution(mesh):
    in_specs = (P("row", "col", None), P("row", "col", None)) + (P(),) * 9
    out_specs = (P("row", "col", None), P("row", "col", None), P(), P())
    return jax.shard_map(shards, mesh=mesh, in_specs=in_specs, out_specs=out_specs, check_vma=False)
```

```python
import jax
import jax.numpy as jnp
import numpy as np
from jax import lax
from jax.experimental import pallas as pl
from jax.experimental.pallas import tpu as pltpu
from jax.sharding import PartitionSpec as P

BOTH = ("row", "col")
SWAP = [(0, 1), (1, 0), (2, 3), (3, 2), (4, 5), (5, 4), (6, 7), (7, 6)]
ROWS, COLS, WIDTH = 18, 72, 128
ROW_N, COL_N = 32, 8
DEVICES = ROW_N * COL_N
HALF = ROWS // 2
PIECE = HALF * COLS
WIRE = 768
LANES = 2 * WIRE
TOTAL = ROW_N * ROWS
GROUP = ROW_N // COL_N
STEP = 256
F32, BF16 = jnp.float32, jnp.bfloat16


def one_hot(targets, length):
    table = np.zeros((len(targets), length), np.float32)
    table[np.arange(len(targets)), targets] = 1
    return jnp.asarray(table, BF16)


def tables():
    col, row = np.divmod(np.arange(DEVICES), ROW_N)
    by_col = one_hot(row * COL_N + col, DEVICES)
    row, col = np.divmod(np.arange(DEVICES), COL_N)
    by_row = one_hot(col * ROW_N + row, DEVICES)
    half, channel = np.divmod(np.arange(DEVICES), WIDTH)
    by_half = one_hot(channel * 2 + half, DEVICES)
    channel, half = np.divmod(np.arange(DEVICES), 2)
    by_channel = one_hot(half * WIDTH + channel, DEVICES)
    place, row = np.divmod(np.arange(TOTAL), ROW_N)
    col, part = np.divmod(row, GROUP)
    spread = one_hot(col * 128 + part * ROWS + place, COL_N * 128)
    return by_col, by_row, by_half, by_channel, spread


PLAIN = ((1,), (0,))
LAST = ((1,), (1,))


def dot(a, b, contract=PLAIN):
    return lax.dot_general(a, b, (contract, ((), ())), preferred_element_type=F32)


def split(x):
    high = x.astype(BF16)
    return high, (x - high.astype(F32)).astype(BF16)


def fine(a, b, contract=PLAIN):
    return dot(a[0], b[0], contract) + (dot(a[0], b[1], contract) + dot(a[1], b[0], contract))


def move(table, values):
    return dot(table[...], values).astype(BF16)


def sigmoid(x):
    return 0.5 * jnp.tanh(0.5 * x) + 0.5


def normalise(values):
    centred = values - jnp.mean(values, axis=0, keepdims=True)
    spread = jnp.mean(centred * centred, axis=0, keepdims=True)
    scale = lax.rsqrt(spread + 1e-05)
    return centred * scale, scale


def normalise_back(d_hat, hat, scale):
    return scale * (
        d_hat
        - jnp.mean(d_hat, axis=0, keepdims=True)
        - hat * jnp.mean(d_hat * hat, axis=0, keepdims=True)
    )


def column(ref):
    return jnp.broadcast_to(ref[...], (8, WIDTH)).T[:, :1]


def columns(ref):
    table = jnp.concatenate([ref[...], jnp.zeros((3, WIDTH), F32)], axis=0).T
    return [table[:, i : i + 1] for i in range(5)]


def fill(padded, block):
    for half in range(2):
        padded[pl.ds(half * WIRE, PIECE), :] = block[pl.ds(half * PIECE, PIECE), :]
        padded[pl.ds(half * WIRE + PIECE, WIRE - PIECE), :] = jnp.zeros(
            (WIRE - PIECE, WIDTH), F32
        )


def drain(block, padded):
    for half in range(2):
        block[pl.ds(half * PIECE, PIECE), :] = padded[pl.ds(half * WIRE, PIECE), :]


def place_of(step):
    per = WIRE // STEP
    half = step // per
    return (
        pl.ds(pl.multiple_of(half * WIDTH, WIDTH), WIDTH),
        pl.ds(pl.multiple_of((step - half * per) * STEP, STEP), STEP),
    )


def lanes_of(step):
    return pl.ds(pl.multiple_of(step * STEP, STEP), STEP)


def build_mask(place, valid, mask):
    values = jnp.concatenate([valid[...].astype(F32), jnp.zeros((1, WIRE - TOTAL), F32)], axis=1)
    values = jnp.broadcast_to(values, (8, WIRE))
    lane = lax.broadcasted_iota(jnp.int32, (8, WIRE), 1)

    def window(start):
        return pltpu.roll(values, jnp.where(start == 0, 0, WIRE - start), 1)

    cols = jnp.where(lane < COLS, window(place[1] * COLS), 0.0)
    rows = window(place[0] * ROWS)
    shifted = [cols] + [pltpu.roll(cols, i * COLS, 1) for i in range(1, HALF)]
    for half in range(2):
        total = jnp.zeros((8, WIRE), F32)
        for i in range(HALF):
            row = half * HALF + i
            total = total + rows[:, row : row + 1] * shifted[i]
        mask[:, half * WIRE : (half + 1) * WIRE] = total[:1]


def project_kernel(
    place, valid, pair, weight, bias, gain, shift, by_channel,
    wire, mask,
    padded, left_s, right_s,
):
    build_mask(place, valid, mask)
    fill(padded, pair)
    gain_c, shift_c = column(gain), column(shift)
    bias_c = jnp.concatenate(columns(bias)[:4], axis=0)
    weight_t = split(weight[:, : 4 * WIDTH].T)

    @pl.loop(0, LANES // STEP)
    def _(step):
        lanes = lanes_of(step)
        hat, _ = normalise(padded[lanes, :].T)
        hidden = fine(weight_t, split(hat * gain_c + shift_c)) + bias_c
        valid = mask[:, lanes]
        rows, cols = place_of(step)
        left = valid * sigmoid(hidden[WIDTH : 2 * WIDTH]) * hidden[:WIDTH]
        left_s[rows, cols] = left.astype(BF16)
        right = valid * sigmoid(hidden[3 * WIDTH : 4 * WIDTH]) * hidden[2 * WIDTH : 3 * WIDTH]
        right_s[rows, cols] = right.astype(BF16)

    wire[:, :WIRE] = move(by_channel, left_s[...])
    wire[:, WIRE:] = move(by_channel, right_s[...])


def prepare_kernel(
    mask, pair, cotangent, weight, bias, gain, shift, out_gain, out_weight,
    hat_o, scale_o, factors, opened_o, d_result_o, d_hat_o,
    padded, padded_c,
):
    fill(padded, pair)
    fill(padded_c, cotangent)
    gain_c, shift_c, out_gain_c = column(gain), column(shift), column(out_gain)
    bias_c = jnp.concatenate(columns(bias), axis=0)
    weight_t = split(weight[...].T)
    out_w = split(out_weight[...])

    @pl.loop(0, LANES // STEP)
    def _(step):
        lanes = lanes_of(step)
        hat, scale = normalise(padded[lanes, :].T)
        hat_o[:, lanes] = hat
        scale_o[:, lanes] = scale
        hidden = fine(weight_t, split(hat * gain_c + shift_c)) + bias_c
        valid = mask[:, lanes]
        for i in range(2):
            opened = sigmoid(hidden[(2 * i + 1) * WIDTH : (2 * i + 2) * WIDTH])
            factor = valid * opened
            factors[2 * i * WIDTH : (2 * i + 1) * WIDTH, lanes] = factor
            factors[(2 * i + 1) * WIDTH : (2 * i + 2) * WIDTH, lanes] = (
                factor * (1.0 - opened) * hidden[2 * i * WIDTH : (2 * i + 1) * WIDTH]
            )
        opened = sigmoid(hidden[4 * WIDTH :])
        opened_o[:, lanes] = opened
        d_result = padded_c[lanes, :].T * opened
        d_result_o[:, lanes] = d_result
        d_hat_o[:, lanes] = fine(out_w, split(d_result)) * out_gain_c


def unpack(values, out, base):
    keep = lax.broadcasted_iota(jnp.int32, (DEVICES, 128), 1) < COLS
    for i in range(HALF):
        tile, offset = divmod(i * COLS, 128)
        part = values[:, tile * 128 : tile * 128 + 256]
        if offset:
            part = pltpu.roll(part, 256 - offset, 1)
        part = jnp.where(keep, part[:, :128], 0.0).astype(BF16)
        for q in range(COL_N):
            out[pl.ds(base + i * ROW_N, ROW_N), q * 128 : (q + 1) * 128] = part[
                q * ROW_N : (q + 1) * ROW_N
            ]


def pack(values, out):
    out[...] = jnp.zeros_like(out)
    for i in range(HALF):
        tile, offset = divmod(i * COLS, 128)
        part = jnp.concatenate(
            [
                values[i * ROW_N : (i + 1) * ROW_N, q * 128 : (q + 1) * 128]
                for q in range(COL_N)
            ],
            axis=0,
        )
        part = jnp.concatenate([part, jnp.zeros_like(part)], axis=1)
        if offset:
            part = pltpu.roll(part, offset, 1)
        out[:, tile * 128 : tile * 128 + 256] += part


def mix_kernel(place, both_w, other_w, by_col, by_row, spread, wire, left_m, right_m, packed):
    own = place[2] * (TOTAL // 2)
    away = (TOTAL // 2) - own
    unpack(dot(by_col[...], both_w[:, :WIRE]), left_m, 0)
    unpack(dot(by_col[...], both_w[:, WIRE:]), right_m, pl.multiple_of(own, 32))
    unpack(dot(by_col[...], other_w[...]), right_m, pl.multiple_of(away, 32))
    mixed = dot(left_m[...], right_m[...], LAST).astype(BF16)
    pack(dot(mixed, spread[...]), packed)
    wire[...] = move(by_row, packed[...].astype(BF16))


def turn_kernel(mixed_w, d_hat, by_half, by_channel, wire, hat_o, mixed_s, d_mixed_s):
    mixed_s[...] = dot(by_half[...], mixed_w[...])

    @pl.loop(0, LANES // STEP)
    def _(step):
        lanes = lanes_of(step)
        rows, cols = place_of(step)
        hat, scale = normalise(mixed_s[rows, cols])
        hat_o[:, lanes] = hat
        d_mixed_s[rows, cols] = normalise_back(d_hat[:, lanes], hat, scale).astype(BF16)

    wire[...] = move(by_channel, d_mixed_s[...])


def update_kernel(
    hat_m, opened, d_result, hat, weight, gain, shift, out_gain, out_shift, out_weight, out_bias,
    update, grad_out, grad_gate, d_normed,
    padded,
):
    gain_c, shift_c = column(gain), column(shift)
    out_gain_c, out_shift_c, out_bias_c = column(out_gain), column(out_shift), column(out_bias)
    out_t = split(out_weight[...].T)
    gate_w = split(weight[:, 4 * WIDTH :])
    grad_out[...] = jnp.zeros_like(grad_out)
    grad_gate[...] = jnp.zeros_like(grad_gate)

    @pl.loop(0, LANES // STEP)
    def _(step):
        lanes = lanes_of(step)
        normed = split(hat_m[:, lanes] * out_gain_c + out_shift_c)
        result = fine(out_t, normed) + out_bias_c
        is_open = opened[:, lanes]
        padded[lanes, :] = (is_open * result).T
        given = d_result[:, lanes]
        grad_out[...] += fine(normed, split(given), LAST)
        d_gate = split(given * result * (1.0 - is_open))
        grad_gate[...] += fine(split(hat[:, lanes] * gain_c + shift_c), d_gate, LAST)
        d_normed[:, lanes] = fine(gate_w, d_gate)

    drain(update, padded)


def unmix_kernel(
    place, d_w, left_m, right_m, by_col, by_row, spread,
    left_wire, own_wire, away_wire,
    d_mixed_m, terms, packed,
):
    own = place[2] * (TOTAL // 2)
    away = (TOTAL // 2) - own
    unpack(dot(by_col[...], d_w[...]), d_mixed_m, 0)
    d_mixed = dot(d_mixed_m[...], spread[...], LAST).astype(BF16)
    terms[...] = dot(d_mixed, left_m[...], ((0,), (0,)))
    pack(terms[pl.ds(pl.multiple_of(away, 32), TOTAL // 2), :], packed)
    away_wire[...] = move(by_row, packed[...].astype(BF16))
    pack(terms[pl.ds(pl.multiple_of(own, 32), TOTAL // 2), :], packed)
    own_wire[...] = move(by_row, packed[...].astype(BF16))
    pack(dot(d_mixed, right_m[...]), packed)
    left_wire[...] = move(by_row, packed[...].astype(BF16))


def d_hidden_of(d_left_s, d_right_s, factors, step):
    rows, cols = place_of(step)
    lanes = lanes_of(step)
    parts = []
    for i, ref in enumerate((d_left_s, d_right_s)):
        given = ref[rows, cols]
        for j in range(2):
            start = (2 * i + j) * WIDTH
            parts.append(given * factors[start : start + WIDTH, lanes])
    return split(jnp.concatenate(parts, axis=0))


def weight_kernel(
    both_w, factors, hat, gain, shift, grad_gate, grad_out, by_half,
    grads,
    d_left_s, d_right_s, total,
):
    d_left_s[...] = dot(by_half[...], both_w[:, :WIRE])
    d_right_s[...] = dot(by_half[...], both_w[:, WIRE:])
    gain_c, shift_c = column(gain), column(shift)
    total[...] = jnp.zeros_like(total)

    @pl.loop(0, LANES // STEP)
    def _(step):
        d_hidden = d_hidden_of(d_left_s, d_right_s, factors, step)
        normed = split(hat[:, lanes_of(step)] * gain_c + shift_c)
        total[...] += fine(normed, d_hidden, LAST)

    grads[:WIDTH, :] = total[:, : 3 * WIDTH].astype(BF16)
    grads[WIDTH:, :WIDTH] = total[:, 3 * WIDTH :].astype(BF16)
    grads[WIDTH:, WIDTH : 2 * WIDTH] = grad_gate[...].astype(BF16)
    grads[WIDTH:, 2 * WIDTH :] = grad_out[...].astype(BF16)


def pair_kernel(
    both_w, factors, hat, scale, d_normed, weight, gain, by_half,
    grad_pair,
    d_left_s, d_right_s, padded,
):
    d_left_s[...] = dot(by_half[...], both_w[:, :WIRE])
    d_right_s[...] = dot(by_half[...], both_w[:, WIRE:])
    gain_c = column(gain)
    weight_s = split(weight[:, : 4 * WIDTH])

    @pl.loop(0, LANES // STEP)
    def _(step):
        lanes = lanes_of(step)
        d_hidden = d_hidden_of(d_left_s, d_right_s, factors, step)
        d_hat = (fine(weight_s, d_hidden) + d_normed[:, lanes]) * gain_c
        padded[lanes, :] = normalise_back(d_hat, hat[:, lanes], scale[:, lanes]).T

    drain(grad_pair, padded)


def call(kernel, outs, scratch, *args, smem=0, work=2e9, room=48):
    whole = lambda shape: pl.BlockSpec(shape, lambda i: (0,) * len(shape))
    scalars = [pl.BlockSpec(memory_space=pltpu.SMEM)] * smem
    return pl.pallas_call(
        kernel,
        grid=(1,),
        out_shape=[jax.ShapeDtypeStruct(*o) for o in outs],
        in_specs=scalars + [whole(a.shape) for a in args[smem:]],
        out_specs=[whole(o[0]) for o in outs],
        scratch_shapes=[pltpu.VMEM(*s) for s in scratch],
        compiler_params=pltpu.CompilerParams(vmem_limit_bytes=room * 2**20),
        cost_estimate=pl.CostEstimate(flops=int(work), bytes_accessed=4 * 2**20, transcendentals=0),
    )(*args)


def spin(step, count, inner):
    size = 32 if inner != 2 else 8
    return [
        (i, i - (i // inner % count) * inner + ((i // inner + step) % count) * inner)
        for i in range(size)
    ]


def meet(value, axis, count, inner):
    value = lax.optimization_barrier(value.astype(BF16))
    others = [lax.ppermute(value, axis, spin(k, count, inner)) for k in range(1, count)]
    own = value.astype(F32)
    if count == 2:
        return own + others[0].astype(F32)
    one, two, three = (o.astype(F32) for o in others)
    return (own + two) + (one + three)


def sum_over_devices(grads, row, col, beside):
    core, x = col % 2, row % 4
    pick = lambda a, i: lax.dynamic_index_in_dim(a, i, 0, keepdims=False)
    pairs = grads.reshape(2, WIDTH, 3 * WIDTH)
    taken = lax.ppermute(pick(pairs, 1 - core), "col", SWAP)
    total = pick(pairs, core).astype(F32) + taken.astype(F32)
    total = total.astype(BF16).reshape(4, WIDTH // 4, 3 * WIDTH)
    taken = [
        lax.ppermute(pick(total, (x + k) % 4), "row", spin(k, 4, 1)).astype(F32) for k in (1, 2, 3)
    ]
    total = (pick(total, x).astype(F32) + taken[0]) + (taken[1] + taken[2])
    total = meet(total, "row", 4, 8)
    total = meet(total, "col", 4, 2)
    total, beside = lax.optimization_barrier((meet(total, "row", 2, 4).astype(BF16), beside))
    parts = jnp.zeros((4, WIDTH // 4, 3 * WIDTH), BF16)
    parts = lax.dynamic_update_index_in_dim(parts, total, x, 0)
    for k in (1, 2, 3):
        taken = lax.ppermute(total, "row", spin(k, 4, 1))
        parts = lax.dynamic_update_index_in_dim(parts, taken, (x + 4 - k) % 4, 0)
    parts = parts.reshape(WIDTH, 3 * WIDTH)
    other = lax.ppermute(parts, "col", SWAP)
    first = core == 0
    upper, lower = jnp.where(first, parts, other), jnp.where(first, other, parts)
    return upper.astype(F32), lower.astype(F32), beside


def exchange(chunks):
    return lax.all_to_all(chunks, BOTH, 0, 0, tiled=True)


def shards(
    pair,
    cotangent,
    residue_mask,
    ln_gain,
    ln_bias,
    proj_weight,
    proj_bias,
    norm_gain,
    norm_bias,
    out_weight,
    out_bias,
):
    by_col, by_row, by_half, by_channel, spread = tables()
    shape = pair.shape
    places = ROWS * COLS
    row, col = lax.axis_index("row"), lax.axis_index("col")
    place = jnp.stack([row, col, col % 2]).astype(jnp.int32)
    pair = pair.reshape(places, WIDTH)
    cotangent = cotangent.reshape(places, WIDTH)
    line = lambda v: v.reshape(-1, WIDTH)
    gain, shift, bias = line(ln_gain), line(ln_bias), line(proj_bias)
    out_gain, out_shift, out_bias = line(norm_gain), line(norm_bias), line(out_bias)
    whole = ((LANES, WIDTH), F32)
    turned = ((WIDTH, LANES), F32)
    square = ((WIDTH, WIDTH), F32)
    halves = lambda kind: ((DEVICES, WIRE), kind)

    wire, mask = call(
        project_kernel,
        [((DEVICES, LANES), BF16), ((1, LANES), F32)],
        [whole, halves(BF16), halves(BF16)],
        place, residue_mask.reshape(1, TOTAL), pair, proj_weight, bias, gain, shift, by_channel,
        smem=1,
        room=62,
    )
    got = exchange(wire.reshape(DEVICES, 2, WIRE)).reshape(DEVICES, LANES)
    hat, scale, factors, opened, d_result, d_hat = call(
        prepare_kernel,
        [turned, ((1, LANES), F32), ((4 * WIDTH, LANES), F32), turned, turned, turned],
        [whole, whole],
        mask, pair, cotangent, proj_weight, bias, gain, shift, out_gain, out_weight,
        work=1e10,
    )
    other_w = lax.ppermute(got[:, WIRE:], "col", SWAP)
    wire, left_m, right_m = call(
        mix_kernel,
        [halves(BF16), ((TOTAL // 2, COL_N * 128), BF16), ((TOTAL, COL_N * 128), BF16)],
        [halves(F32)],
        place, got, other_w, by_col, by_row, spread,
        smem=1,
    )
    got = exchange(wire.reshape(DEVICES, 2, WIRE // 2)).reshape(DEVICES, WIRE)
    wire, hat_m = call(
        turn_kernel,
        [halves(BF16), turned],
        [halves(F32), halves(BF16)],
        got, d_hat, by_half, by_channel,
    )
    got = exchange(wire.reshape(DEVICES, 2, WIRE // 2)).reshape(DEVICES, WIRE)
    update, grad_out, grad_gate, d_normed = call(
        update_kernel,
        [((places, WIDTH), F32), square, square, turned],
        [whole],
        hat_m, opened, d_result, hat, proj_weight, gain, shift, out_gain, out_shift, out_weight,
        out_bias,
        work=8e9,
    )
    left_wire, own_wire, away_wire = call(
        unmix_kernel,
        [halves(BF16)] * 3,
        [((TOTAL // 2, COL_N * 128), BF16), ((TOTAL, COL_N * 128), F32), halves(F32)],
        place, got, left_m, right_m, by_col, by_row, spread,
        smem=1,
    )
    other_wire = lax.ppermute(away_wire, "col", SWAP)
    right_wire = (own_wire.astype(F32) + other_wire.astype(F32)).astype(BF16)
    got = exchange(jnp.stack([left_wire, right_wire], axis=1)).reshape(DEVICES, LANES)
    (grads,) = call(
        weight_kernel,
        [((DEVICES, 3 * WIDTH), BF16)],
        [halves(F32), halves(F32), ((WIDTH, 4 * WIDTH), F32)],
        got, factors, hat, gain, shift, grad_gate, grad_out, by_half,
    )
    (grad_pair,) = call(
        pair_kernel,
        [((places, WIDTH), F32)],
        [halves(F32), halves(F32), whole],
        got, factors, hat, scale, d_normed, proj_weight, gain, by_half,
        work=8e9,
    )
    upper, lower, grad_pair = sum_over_devices(grads, row, col, grad_pair)
    grad_proj = jnp.concatenate([upper, lower[:, : 2 * WIDTH]], axis=1)
    return update.reshape(shape), grad_pair.reshape(shape), grad_proj, lower[:, 2 * WIDTH :]


def solution(mesh):
    in_specs = (P("row", "col", None), P("row", "col", None)) + (P(),) * 9
    out_specs = (P("row", "col", None), P("row", "col", None), P(), P())
    return jax.shard_map(shards, mesh=mesh, in_specs=in_specs, out_specs=out_specs, check_vma=False)
```

```python
import jax
import jax.numpy as jnp
import numpy as np
from jax import lax
from jax.experimental import pallas as pl
from jax.experimental.pallas import tpu as pltpu
from jax.sharding import PartitionSpec as P

BOTH = ("row", "col")
SWAP = [(0, 1), (1, 0), (2, 3), (3, 2), (4, 5), (5, 4), (6, 7), (7, 6)]
ROWS, COLS, WIDTH = 18, 72, 128
ROW_N, COL_N = 32, 8
DEVICES = ROW_N * COL_N
HALF = ROWS // 2
PIECE = HALF * COLS
WIRE = 768
LANES = 2 * WIRE
TOTAL = ROW_N * ROWS
GROUP = ROW_N // COL_N
STEP = 256
STEPS = LANES // STEP
F32, BF16 = jnp.float32, jnp.bfloat16


def one_hot(targets, length):
    table = np.zeros((len(targets), length), np.float32)
    table[np.arange(len(targets)), targets] = 1
    return jnp.asarray(table, BF16)


def spread_table():
    place, row = np.divmod(np.arange(TOTAL), ROW_N)
    col, part = np.divmod(row, GROUP)
    return one_hot(col * 128 + part * ROWS + place, COL_N * 128)


HAT, OPEN, GIVEN, D_HAT, SAVED = 512, 640, 768, 896, 1024
LEFT_ROWS, KEPT_ROWS, KEPT = 288, 864, 3072
BY_COL, BY_ROW, BY_HALF, BY_CHANNEL = 5, 3, 7, 1


def order(bits):
    n = lax.broadcasted_iota(jnp.int32, (DEVICES, DEVICES), 0)
    target = ((n & ((1 << bits) - 1)) << (8 - bits)) + (n >> bits)
    other = lax.broadcasted_iota(jnp.int32, (DEVICES, DEVICES), 1)
    return jnp.where(other == target, 1.0, 0.0).astype(BF16)


PLAIN = ((1,), (0,))
LAST = ((1,), (1,))


def dot(a, b, contract=PLAIN):
    return lax.dot_general(a, b, (contract, ((), ())), preferred_element_type=F32)


def split(x):
    high = x.astype(BF16)
    return high, (x - high.astype(F32)).astype(BF16)


def fine(a, b, contract=PLAIN):
    return dot(a[0], b[0], contract) + (dot(a[0], b[1], contract) + dot(a[1], b[0], contract))


def move(bits, values):
    return dot(order(bits), values)


def sigmoid(x):
    return 0.5 * jnp.tanh(0.5 * x) + 0.5


def normalise(values):
    centred = values - jnp.mean(values, axis=0, keepdims=True)
    spread = jnp.mean(centred * centred, axis=0, keepdims=True)
    scale = lax.rsqrt(spread + 1e-05)
    return centred * scale, scale


def normalise_back(d_hat, hat, scale):
    return scale * (
        d_hat
        - jnp.mean(d_hat, axis=0, keepdims=True)
        - hat * jnp.mean(d_hat * hat, axis=0, keepdims=True)
    )


def column(ref):
    return jnp.broadcast_to(ref[...], (8, WIDTH)).T[:, :1]


def columns(ref):
    table = jnp.concatenate([ref[...], jnp.zeros((3, WIDTH), F32)], axis=0).T
    return [table[:, i : i + 1] for i in range(5)]


def fill(padded, block):
    for half in range(2):
        padded[pl.ds(half * WIRE, PIECE), :] = block[pl.ds(half * PIECE, PIECE), :]
        padded[pl.ds(half * WIRE + PIECE, WIRE - PIECE), :] = jnp.zeros(
            (WIRE - PIECE, WIDTH), F32
        )


def drain(block, padded):
    for half in range(2):
        block[pl.ds(half * PIECE, PIECE), :] = padded[pl.ds(half * WIRE, PIECE), :]


def place_of(step):
    per = WIRE // STEP
    half = step // per
    return (
        pl.ds(pl.multiple_of(half * WIDTH, WIDTH), WIDTH),
        pl.ds(pl.multiple_of((step - half * per) * STEP, STEP), STEP),
    )


def lanes_of(step):
    return pl.ds(pl.multiple_of(step * STEP, STEP), STEP)


def build_mask(row, col, valid, mask):
    lane = lax.broadcasted_iota(jnp.int32, (8, 128), 1)
    cols = jnp.zeros((8, 128), F32)
    for k in range(COLS):
        cols = jnp.where(lane == k, valid[col * COLS + k].astype(F32), cols)
    cols = jnp.concatenate([cols, jnp.zeros((8, WIRE - 128), F32)], axis=1)
    shifted = [cols] + [pltpu.roll(cols, i * COLS, 1) for i in range(1, HALF)]
    for half in range(2):
        total = jnp.zeros((8, WIRE), F32)
        for i in range(HALF):
            total = total + valid[row * ROWS + half * HALF + i].astype(F32) * shifted[i]
        mask[:, half * WIRE : (half + 1) * WIRE] = total[:1]


def project_kernel(
    valid, pair, weight, bias, gain, shift,
    wire, mask,
    padded, left_s, right_s,
):
    build_mask(lax.axis_index("row"), lax.axis_index("col"), valid, mask)
    fill(padded, pair)
    gain_c, shift_c = column(gain), column(shift)
    bias_c = jnp.concatenate(columns(bias)[:4], axis=0)
    weight_t = split(weight[:, : 4 * WIDTH].T)

    @pl.loop(0, STEPS)
    def _(step):
        lanes = lanes_of(step)
        hat, _ = normalise(padded[lanes, :].T)
        hidden = fine(weight_t, split(hat * gain_c + shift_c)) + bias_c
        valid = mask[:, lanes]
        rows, cols = place_of(step)
        left = valid * sigmoid(hidden[WIDTH : 2 * WIDTH]) * hidden[:WIDTH]
        left_s[rows, cols] = left.astype(BF16)
        right = valid * sigmoid(hidden[3 * WIDTH : 4 * WIDTH]) * hidden[2 * WIDTH : 3 * WIDTH]
        right_s[rows, cols] = right.astype(BF16)

    wire[:, :WIRE] = move(BY_CHANNEL, left_s[...]).astype(BF16)
    wire[:, WIRE:] = move(BY_CHANNEL, right_s[...]).astype(BF16)


def prepare_kernel(
    mask, pair, cotangent, weight, bias, gain, shift, out_gain, out_weight,
    scale_o, saved,
    padded, padded_c, held, sems,
):
    fill(padded, pair)
    fill(padded_c, cotangent)
    gain_c, shift_c, out_gain_c = column(gain), column(shift), column(out_gain)
    bias_c = jnp.concatenate(columns(bias), axis=0)
    weight_t = split(weight[...].T)
    out_w = split(out_weight[...])

    def leave(step):
        lanes = lanes_of(step)
        return pltpu.make_async_copy(held.at[:, lanes], saved.at[:, lanes], sems.at[step])

    @pl.loop(0, STEPS)
    def _(step):
        lanes = lanes_of(step)
        hat, scale = normalise(padded[lanes, :].T)
        held[HAT:OPEN, lanes] = hat
        scale_o[:, lanes] = scale
        hidden = fine(weight_t, split(hat * gain_c + shift_c)) + bias_c
        valid = mask[:, lanes]
        for i in range(2):
            opened = sigmoid(hidden[(2 * i + 1) * WIDTH : (2 * i + 2) * WIDTH])
            factor = valid * opened
            held[2 * i * WIDTH : (2 * i + 1) * WIDTH, lanes] = factor
            held[(2 * i + 1) * WIDTH : (2 * i + 2) * WIDTH, lanes] = (
                factor * (1.0 - opened) * hidden[2 * i * WIDTH : (2 * i + 1) * WIDTH]
            )
        opened = sigmoid(hidden[4 * WIDTH :])
        held[OPEN:GIVEN, lanes] = opened
        d_result = padded_c[lanes, :].T * opened
        held[GIVEN:D_HAT, lanes] = d_result
        held[D_HAT:SAVED, lanes] = fine(out_w, split(d_result)) * out_gain_c
        leave(step).start()

    @pl.loop(0, STEPS)
    def _(step):
        leave(step).wait()


def unpack(values, out, base):
    keep = lax.broadcasted_iota(jnp.int32, (DEVICES, 128), 1) < COLS
    for i in range(HALF):
        tile, offset = divmod(i * COLS, 128)
        part = values[:, tile * 128 : tile * 128 + 256]
        if offset:
            part = pltpu.roll(part, 256 - offset, 1)
        part = jnp.where(keep, part[:, :128], 0.0).astype(BF16)
        for q in range(COL_N):
            out[pl.ds(base + i * ROW_N, ROW_N), q * 128 : (q + 1) * 128] = part[
                q * ROW_N : (q + 1) * ROW_N
            ]


def pack(values, out):
    out[...] = jnp.zeros_like(out)
    for i in range(HALF):
        tile, offset = divmod(i * COLS, 128)
        part = jnp.concatenate(
            [
                values[i * ROW_N : (i + 1) * ROW_N, q * 128 : (q + 1) * 128]
                for q in range(COL_N)
            ],
            axis=0,
        )
        part = jnp.concatenate([part, jnp.zeros_like(part)], axis=1)
        if offset:
            part = pltpu.roll(part, offset, 1)
        out[:, tile * 128 : tile * 128 + 256] += part


def mix_kernel(both_w, other_w, spread, wire, kept, left_m, right_m, packed, sems):
    own = lax.axis_index("col") % 2 * (TOTAL // 2)
    away = (TOTAL // 2) - own
    keep_left = pltpu.make_async_copy(left_m, kept.at[:LEFT_ROWS, :], sems.at[0])
    keep_right = pltpu.make_async_copy(right_m, kept.at[LEFT_ROWS:KEPT_ROWS, :], sems.at[1])
    by_col = order(BY_COL)
    unpack(dot(by_col, both_w[:, :WIRE]), left_m, 0)
    keep_left.start()
    unpack(dot(by_col, both_w[:, WIRE:]), right_m, pl.multiple_of(own, 32))
    unpack(dot(by_col, other_w[...]), right_m, pl.multiple_of(away, 32))
    keep_right.start()
    mixed = dot(left_m[...], right_m[...], LAST).astype(BF16)
    pack(dot(mixed, spread[...]), packed)
    wire[...] = move(BY_ROW, packed[...].astype(BF16)).astype(BF16)
    keep_left.wait()
    keep_right.wait()


def turn_kernel(mixed_w, saved, wire, mixed_s, d_mixed_s, d_hat, sem):
    fetch = pltpu.make_async_copy(saved.at[D_HAT:SAVED, :], d_hat, sem)
    fetch.start()
    mixed_s[...] = move(BY_HALF, mixed_w[...])
    fetch.wait()

    @pl.loop(0, STEPS)
    def _(step):
        rows, cols = place_of(step)
        hat, scale = normalise(mixed_s[rows, cols])
        d_mixed_s[rows, cols] = normalise_back(d_hat[:, lanes_of(step)], hat, scale).astype(BF16)

    wire[...] = move(BY_CHANNEL, d_mixed_s[...]).astype(BF16)


def update_kernel(
    mixed_w, saved, weight, gain, shift, out_gain, out_shift, out_weight, out_bias,
    update, grad_out, grad_gate, d_normed,
    padded, mixed_s, held, sem,
):
    fetch = pltpu.make_async_copy(saved.at[HAT:D_HAT, :], held, sem)
    fetch.start()
    mixed_s[...] = move(BY_HALF, mixed_w[...])
    gain_c, shift_c = column(gain), column(shift)
    out_gain_c, out_shift_c, out_bias_c = column(out_gain), column(out_shift), column(out_bias)
    out_t = split(out_weight[...].T)
    gate_w = split(weight[:, 4 * WIDTH :])
    grad_out[...] = jnp.zeros_like(grad_out)
    grad_gate[...] = jnp.zeros_like(grad_gate)
    fetch.wait()

    @pl.loop(0, STEPS)
    def _(step):
        lanes = lanes_of(step)
        rows, cols = place_of(step)
        hat_m, _ = normalise(mixed_s[rows, cols])
        normed = split(hat_m * out_gain_c + out_shift_c)
        result = fine(out_t, normed) + out_bias_c
        is_open = held[OPEN - HAT : GIVEN - HAT, lanes]
        padded[lanes, :] = (is_open * result).T
        given = held[GIVEN - HAT :, lanes]
        grad_out[...] += fine(normed, split(given), LAST)
        d_gate = split(given * result * (1.0 - is_open))
        grad_gate[...] += fine(
            split(held[: OPEN - HAT, lanes] * gain_c + shift_c), d_gate, LAST
        )
        d_normed[:, lanes] = fine(gate_w, d_gate)

    drain(update, padded)


def unmix_kernel(
    d_w, kept, spread,
    left_wire, own_wire, away_wire,
    d_mixed_m, terms, packed, left_m, right_m, sems,
):
    own = lax.axis_index("col") % 2 * (TOTAL // 2)
    away = (TOTAL // 2) - own
    get_left = pltpu.make_async_copy(kept.at[:LEFT_ROWS, :], left_m, sems.at[0])
    get_right = pltpu.make_async_copy(kept.at[LEFT_ROWS:KEPT_ROWS, :], right_m, sems.at[1])
    get_left.start()
    get_right.start()
    by_row = order(BY_ROW)
    send = lambda: dot(by_row, packed[...].astype(BF16)).astype(BF16)
    unpack(move(BY_COL, d_w[...]), d_mixed_m, 0)
    d_mixed = dot(d_mixed_m[...], spread[...], LAST).astype(BF16)
    get_left.wait()
    terms[...] = dot(d_mixed, left_m[...], ((0,), (0,)))
    pack(terms[pl.ds(pl.multiple_of(away, 32), TOTAL // 2), :], packed)
    away_wire[...] = send()
    pack(terms[pl.ds(pl.multiple_of(own, 32), TOTAL // 2), :], packed)
    own_wire[...] = send()
    get_right.wait()
    pack(dot(d_mixed, right_m[...]), packed)
    left_wire[...] = send()


def d_hidden_of(d_left_s, d_right_s, factors, step):
    rows, cols = place_of(step)
    lanes = lanes_of(step)
    parts = []
    for i, ref in enumerate((d_left_s, d_right_s)):
        given = ref[rows, cols]
        for j in range(2):
            start = (2 * i + j) * WIDTH
            parts.append(given * factors[start : start + WIDTH, lanes])
    return split(jnp.concatenate(parts, axis=0))


def fetch_saved(saved, held, sems, step):
    lanes = lanes_of(step)
    return pltpu.make_async_copy(saved.at[:OPEN, lanes], held.at[:, lanes], sems.at[step])


def weight_kernel(
    both_w, saved, gain, shift, grad_gate, grad_out,
    grads,
    d_left_s, d_right_s, total, held, sems,
):
    for step in range(STEPS):
        fetch_saved(saved, held, sems, step).start()
    by_half = order(BY_HALF)
    d_left_s[...] = dot(by_half, both_w[:, :WIRE])
    d_right_s[...] = dot(by_half, both_w[:, WIRE:])
    gain_c, shift_c = column(gain), column(shift)
    total[...] = jnp.zeros_like(total)

    @pl.loop(0, STEPS)
    def _(step):
        fetch_saved(saved, held, sems, step).wait()
        d_hidden = d_hidden_of(d_left_s, d_right_s, held, step)
        normed = split(held[HAT:OPEN, lanes_of(step)] * gain_c + shift_c)
        total[...] += fine(normed, d_hidden, LAST)

    grads[:WIDTH, :] = total[:, : 3 * WIDTH]
    grads[WIDTH:, :WIDTH] = total[:, 3 * WIDTH :]
    grads[WIDTH:, WIDTH : 2 * WIDTH] = grad_gate[...]
    grads[WIDTH:, 2 * WIDTH :] = grad_out[...]


def pair_kernel(
    both_w, saved, scale, d_normed, weight, gain,
    grad_pair,
    d_left_s, d_right_s, padded, held, sems,
):
    for step in range(STEPS):
        fetch_saved(saved, held, sems, step).start()
    by_half = order(BY_HALF)
    d_left_s[...] = dot(by_half, both_w[:, :WIRE])
    d_right_s[...] = dot(by_half, both_w[:, WIRE:])
    gain_c = column(gain)
    weight_s = split(weight[:, : 4 * WIDTH])

    @pl.loop(0, STEPS)
    def _(step):
        fetch_saved(saved, held, sems, step).wait()
        lanes = lanes_of(step)
        d_hidden = d_hidden_of(d_left_s, d_right_s, held, step)
        d_hat = (fine(weight_s, d_hidden) + d_normed[:, lanes]) * gain_c
        padded[lanes, :] = normalise_back(d_hat, held[HAT:OPEN, lanes], scale[:, lanes]).T

    drain(grad_pair, padded)


class Raw:
    def __init__(self, value):
        self.value = value


def call(kernel, outs, scratch, *args, smem=0, work=2e9, room=48):
    operands = [a.value if isinstance(a, Raw) else a for a in args]
    results = [jax.ShapeDtypeStruct(*(o.value if isinstance(o, Raw) else o)) for o in outs]

    def spec(value, raw):
        if raw:
            return pl.BlockSpec(memory_space=pl.ANY)
        return pl.BlockSpec(value.shape, lambda i: (0,) * len(value.shape))

    specs = [spec(v, isinstance(w, Raw)) for v, w in zip([*operands, *results], [*args, *outs])]
    specs[:smem] = [pl.BlockSpec(memory_space=pltpu.SMEM)] * smem
    return pl.pallas_call(
        kernel,
        grid=(1,),
        out_shape=results,
        in_specs=specs[: len(args)],
        out_specs=specs[len(args) :],
        scratch_shapes=[pltpu.VMEM(*s) if isinstance(s, tuple) else s for s in scratch],
        compiler_params=pltpu.CompilerParams(vmem_limit_bytes=room * 2**20),
        cost_estimate=pl.CostEstimate(flops=int(work), bytes_accessed=4 * 2**20, transcendentals=0),
    )(*operands)


def spin(step, count, inner):
    size = 32 if inner != 2 else 8
    return [
        (i, i - (i // inner % count) * inner + ((i // inner + step) % count) * inner)
        for i in range(size)
    ]


def meet(value, axis, count, inner):
    others = [lax.ppermute(value, axis, spin(k, count, inner)) for k in range(1, count)]
    if count == 2:
        return value + others[0]
    one, two, three = others
    return (value + two) + (one + three)


def sum_over_devices(grads, row, col, beside):
    core, x = col % 2, row % 4
    pick = lambda a, i: lax.dynamic_index_in_dim(a, i, 0, keepdims=False)
    pairs = grads.reshape(2, WIDTH, 3 * WIDTH)
    taken = lax.ppermute(pick(pairs, 1 - core), "col", SWAP)
    total = pick(pairs, core) + taken
    total = total.astype(BF16).reshape(4, WIDTH // 4, 3 * WIDTH)
    taken = [
        lax.ppermute(pick(total, (x + k) % 4), "row", spin(k, 4, 1)).astype(F32) for k in (1, 2, 3)
    ]
    total = (pick(total, x).astype(F32) + taken[0]) + (taken[1] + taken[2])
    total = meet(total, "row", 4, 8)
    total = meet(total, "col", 4, 2)
    total, beside = lax.optimization_barrier((meet(total, "row", 2, 4).astype(BF16), beside))
    parts = jnp.zeros((4, WIDTH // 4, 3 * WIDTH), BF16)
    parts = lax.dynamic_update_index_in_dim(parts, total, x, 0)
    for k in (1, 2, 3):
        taken = lax.ppermute(total, "row", spin(k, 4, 1))
        parts = lax.dynamic_update_index_in_dim(parts, taken, (x + 4 - k) % 4, 0)
    parts = parts.reshape(WIDTH, 3 * WIDTH)
    other = lax.ppermute(parts, "col", SWAP)
    first = core == 0
    upper, lower = jnp.where(first, parts, other), jnp.where(first, other, parts)
    return upper.astype(F32), lower.astype(F32), beside


def exchange(chunks):
    return lax.all_to_all(chunks, BOTH, 0, 0, tiled=True)


def shards(
    pair,
    cotangent,
    residue_mask,
    ln_gain,
    ln_bias,
    proj_weight,
    proj_bias,
    norm_gain,
    norm_bias,
    out_weight,
    out_bias,
):
    spread = spread_table()
    shape = pair.shape
    places = ROWS * COLS
    row, col = lax.axis_index("row"), lax.axis_index("col")
    pair = pair.reshape(places, WIDTH)
    cotangent = cotangent.reshape(places, WIDTH)
    line = lambda v: v.reshape(-1, WIDTH)
    gain, shift, bias = line(ln_gain), line(ln_bias), line(proj_bias)
    out_gain, out_shift, out_bias = line(norm_gain), line(norm_bias), line(out_bias)
    whole = ((LANES, WIDTH), F32)
    turned = ((WIDTH, LANES), F32)
    square = ((WIDTH, WIDTH), F32)
    halves = lambda kind: ((DEVICES, WIRE), kind)

    wire, mask = call(
        project_kernel,
        [((DEVICES, LANES), BF16), ((1, LANES), F32)],
        [whole, halves(BF16), halves(BF16)],
        residue_mask, pair, proj_weight, bias, gain, shift,
        smem=1,
        room=62,
    )
    got = exchange(wire.reshape(DEVICES, 2, WIRE)).reshape(DEVICES, LANES)
    dma = pltpu.SemaphoreType.DMA
    scale, saved = call(
        prepare_kernel,
        [((1, LANES), F32), Raw(((SAVED, LANES), F32))],
        [whole, whole, ((SAVED, LANES), F32), dma((STEPS,))],
        mask, pair, cotangent, proj_weight, bias, gain, shift, out_gain, out_weight,
        work=1e10,
    )
    other_w = lax.ppermute(got[:, WIRE:], "col", SWAP)
    left_s, right_s = ((LEFT_ROWS, COL_N * 128), BF16), ((TOTAL, COL_N * 128), BF16)
    wire, kept = call(
        mix_kernel,
        [halves(BF16), Raw(((KEPT, COL_N * 128), BF16))],
        [left_s, right_s, halves(F32), dma((2,))],
        got, other_w, spread,
    )
    mixed_w = exchange(wire.reshape(DEVICES, 2, WIRE // 2)).reshape(DEVICES, WIRE)
    (wire,) = call(
        turn_kernel,
        [halves(BF16)],
        [halves(F32), halves(BF16), turned, dma],
        mixed_w, Raw(saved),
    )
    got = exchange(wire.reshape(DEVICES, 2, WIRE // 2)).reshape(DEVICES, WIRE)
    update, grad_out, grad_gate, d_normed = call(
        update_kernel,
        [((places, WIDTH), F32), square, square, turned],
        [whole, halves(F32), ((D_HAT - HAT, LANES), F32), dma],
        mixed_w, Raw(saved), proj_weight, gain, shift, out_gain, out_shift, out_weight, out_bias,
        work=8e9,
    )
    left_wire, own_wire, away_wire = call(
        unmix_kernel,
        [halves(BF16)] * 3,
        [left_s, ((TOTAL, COL_N * 128), F32), halves(F32), left_s, right_s, dma((2,))],
        got, Raw(kept), spread,
    )
    other_wire = lax.ppermute(away_wire, "col", SWAP)
    right_wire = (own_wire.astype(F32) + other_wire.astype(F32)).astype(BF16)
    got = exchange(jnp.stack([left_wire, right_wire], axis=1)).reshape(DEVICES, LANES)
    held = ((OPEN, LANES), F32)
    (grads,) = call(
        weight_kernel,
        [((DEVICES, 3 * WIDTH), F32)],
        [halves(F32), halves(F32), ((WIDTH, 4 * WIDTH), F32), held, dma((STEPS,))],
        got, Raw(saved), gain, shift, grad_gate, grad_out,
    )
    (grad_pair,) = call(
        pair_kernel,
        [((places, WIDTH), F32)],
        [halves(F32), halves(F32), whole, held, dma((STEPS,))],
        got, Raw(saved), scale, d_normed, proj_weight, gain,
        work=8e9,
    )
    upper, lower, grad_pair = sum_over_devices(grads, row, col, grad_pair)
    grad_proj = jnp.concatenate([upper, lower[:, : 2 * WIDTH]], axis=1)
    return update.reshape(shape), grad_pair.reshape(shape), grad_proj, lower[:, 2 * WIDTH :]


def solution(mesh):
    in_specs = (P("row", "col", None), P("row", "col", None)) + (P(),) * 9
    out_specs = (P("row", "col", None), P("row", "col", None), P(), P())
    return jax.shard_map(shards, mesh=mesh, in_specs=in_specs, out_specs=out_specs, check_vma=False)
```

```python
import jax
import jax.numpy as jnp
import numpy as np
from jax import lax
from jax.experimental import pallas as pl
from jax.experimental.pallas import tpu as pltpu
from jax.sharding import PartitionSpec as P

BOTH = ("row", "col")
SWAP = [(0, 1), (1, 0), (2, 3), (3, 2), (4, 5), (5, 4), (6, 7), (7, 6)]
ROWS, COLS, WIDTH = 18, 72, 128
ROW_N, COL_N = 32, 8
DEVICES = ROW_N * COL_N
HALF = ROWS // 2
PIECE = HALF * COLS
WIRE = 768
LANES = 2 * WIRE
TOTAL = ROW_N * ROWS
GROUP = ROW_N // COL_N
STEP = 256
STEPS = LANES // STEP
F32, BF16 = jnp.float32, jnp.bfloat16


def one_hot(targets, length):
    table = np.zeros((len(targets), length), np.float32)
    table[np.arange(len(targets)), targets] = 1
    return jnp.asarray(table, BF16)


def spread_table():
    place, row = np.divmod(np.arange(TOTAL), ROW_N)
    col, part = np.divmod(row, GROUP)
    return one_hot(col * 128 + part * ROWS + place, COL_N * 128)


HAT, OPEN, GIVEN, D_HAT, SAVED = 512, 640, 768, 896, 1024
LEFT_ROWS, KEPT_ROWS, KEPT = 288, 864, 3072
BY_COL, BY_ROW, BY_HALF, BY_CHANNEL = 5, 3, 7, 1


def order(bits):
    n = lax.broadcasted_iota(jnp.int32, (DEVICES, DEVICES), 0)
    target = ((n & ((1 << bits) - 1)) << (8 - bits)) + (n >> bits)
    other = lax.broadcasted_iota(jnp.int32, (DEVICES, DEVICES), 1)
    return jnp.where(other == target, 1.0, 0.0).astype(BF16)


PLAIN = ((1,), (0,))
LAST = ((1,), (1,))


def dot(a, b, contract=PLAIN):
    return lax.dot_general(a, b, (contract, ((), ())), preferred_element_type=F32)


def split(x):
    high = x.astype(BF16)
    return high, (x - high.astype(F32)).astype(BF16)


def fine(a, b, contract=PLAIN):
    return dot(a[0], b[0], contract) + (dot(a[0], b[1], contract) + dot(a[1], b[0], contract))


def move(bits, values):
    return dot(order(bits), values)


def sigmoid(x):
    return 0.5 * jnp.tanh(0.5 * x) + 0.5


def normalise(values):
    centred = values - jnp.mean(values, axis=0, keepdims=True)
    spread = jnp.mean(centred * centred, axis=0, keepdims=True)
    scale = lax.rsqrt(spread + 1e-05)
    return centred * scale, scale


def normalise_back(d_hat, hat, scale):
    return scale * (
        d_hat
        - jnp.mean(d_hat, axis=0, keepdims=True)
        - hat * jnp.mean(d_hat * hat, axis=0, keepdims=True)
    )


def column(ref):
    return jnp.broadcast_to(ref[...], (8, WIDTH)).T[:, :1]


def columns(ref):
    table = jnp.concatenate([ref[...], jnp.zeros((3, WIDTH), F32)], axis=0).T
    return [table[:, i : i + 1] for i in range(5)]


def fill(padded, block):
    for half in range(2):
        padded[pl.ds(half * WIRE, PIECE), :] = block[pl.ds(half * PIECE, PIECE), :]
        padded[pl.ds(half * WIRE + PIECE, WIRE - PIECE), :] = jnp.zeros(
            (WIRE - PIECE, WIDTH), F32
        )


def drain(block, padded):
    for half in range(2):
        block[pl.ds(half * PIECE, PIECE), :] = padded[pl.ds(half * WIRE, PIECE), :]


def place_of(step):
    per = WIRE // STEP
    half = step // per
    return (
        pl.ds(pl.multiple_of(half * WIDTH, WIDTH), WIDTH),
        pl.ds(pl.multiple_of((step - half * per) * STEP, STEP), STEP),
    )


def lanes_of(step):
    return pl.ds(pl.multiple_of(step * STEP, STEP), STEP)


def build_mask(row, col, valid, mask):
    lane = lax.broadcasted_iota(jnp.int32, (8, 128), 1)
    cols = jnp.zeros((8, 128), F32)
    for k in range(COLS):
        cols = jnp.where(lane == k, valid[col * COLS + k].astype(F32), cols)
    cols = jnp.concatenate([cols, jnp.zeros((8, WIRE - 128), F32)], axis=1)
    shifted = [cols] + [pltpu.roll(cols, i * COLS, 1) for i in range(1, HALF)]
    for half in range(2):
        total = jnp.zeros((8, WIRE), F32)
        for i in range(HALF):
            total = total + valid[row * ROWS + half * HALF + i].astype(F32) * shifted[i]
        mask[:, half * WIRE : (half + 1) * WIRE] = total[:1]


def project_kernel(
    valid, pair, weight, bias, gain, shift,
    wire, mask,
    padded, left_s, right_s,
):
    build_mask(lax.axis_index("row"), lax.axis_index("col"), valid, mask)
    fill(padded, pair)
    gain_c, shift_c = column(gain), column(shift)
    bias_c = jnp.concatenate(columns(bias)[:4], axis=0)
    weight_t = split(weight[:, : 4 * WIDTH].T)

    @pl.loop(0, STEPS)
    def _(step):
        lanes = lanes_of(step)
        hat, _ = normalise(padded[lanes, :].T)
        hidden = fine(weight_t, split(hat * gain_c + shift_c)) + bias_c
        valid = mask[:, lanes]
        rows, cols = place_of(step)
        left = valid * sigmoid(hidden[WIDTH : 2 * WIDTH]) * hidden[:WIDTH]
        left_s[rows, cols] = left.astype(BF16)
        right = valid * sigmoid(hidden[3 * WIDTH : 4 * WIDTH]) * hidden[2 * WIDTH : 3 * WIDTH]
        right_s[rows, cols] = right.astype(BF16)

    wire[:, :WIRE] = move(BY_CHANNEL, left_s[...]).astype(BF16)
    wire[:, WIRE:] = move(BY_CHANNEL, right_s[...]).astype(BF16)


def prepare_kernel(
    mask, pair, cotangent, weight, bias, gain, shift, out_gain, out_weight,
    scale_o, saved,
    padded, padded_c, held, sems,
):
    fill(padded, pair)
    fill(padded_c, cotangent)
    gain_c, shift_c, out_gain_c = column(gain), column(shift), column(out_gain)
    bias_c = jnp.concatenate(columns(bias), axis=0)
    weight_t = split(weight[...].T)
    out_w = split(out_weight[...])

    def leave(step):
        lanes = lanes_of(step)
        return pltpu.make_async_copy(held.at[:, lanes], saved.at[:, lanes], sems.at[step])

    @pl.loop(0, STEPS)
    def _(step):
        lanes = lanes_of(step)
        hat, scale = normalise(padded[lanes, :].T)
        held[HAT:OPEN, lanes] = hat
        scale_o[:, lanes] = scale
        hidden = fine(weight_t, split(hat * gain_c + shift_c)) + bias_c
        valid = mask[:, lanes]
        for i in range(2):
            opened = sigmoid(hidden[(2 * i + 1) * WIDTH : (2 * i + 2) * WIDTH])
            factor = valid * opened
            held[2 * i * WIDTH : (2 * i + 1) * WIDTH, lanes] = factor
            held[(2 * i + 1) * WIDTH : (2 * i + 2) * WIDTH, lanes] = (
                factor * (1.0 - opened) * hidden[2 * i * WIDTH : (2 * i + 1) * WIDTH]
            )
        opened = sigmoid(hidden[4 * WIDTH :])
        held[OPEN:GIVEN, lanes] = opened
        d_result = padded_c[lanes, :].T * opened
        held[GIVEN:D_HAT, lanes] = d_result
        held[D_HAT:SAVED, lanes] = fine(out_w, split(d_result)) * out_gain_c
        leave(step).start()

    @pl.loop(0, STEPS)
    def _(step):
        leave(step).wait()


def unpack(values, out, base):
    keep = lax.broadcasted_iota(jnp.int32, (DEVICES, 128), 1) < COLS
    for i in range(HALF):
        tile, offset = divmod(i * COLS, 128)
        part = values[:, tile * 128 : tile * 128 + 256]
        if offset:
            part = pltpu.roll(part, 256 - offset, 1)
        part = jnp.where(keep, part[:, :128], 0.0).astype(BF16)
        for q in range(COL_N):
            out[pl.ds(base + i * ROW_N, ROW_N), q * 128 : (q + 1) * 128] = part[
                q * ROW_N : (q + 1) * ROW_N
            ]


def pack(values, out):
    out[...] = jnp.zeros_like(out)
    for i in range(HALF):
        tile, offset = divmod(i * COLS, 128)
        part = jnp.concatenate(
            [
                values[i * ROW_N : (i + 1) * ROW_N, q * 128 : (q + 1) * 128]
                for q in range(COL_N)
            ],
            axis=0,
        )
        part = jnp.concatenate([part, jnp.zeros_like(part)], axis=1)
        if offset:
            part = pltpu.roll(part, offset, 1)
        out[:, tile * 128 : tile * 128 + 256] += part


def mix_kernel(both_w, other_w, spread, wire, kept, left_m, right_m, packed, sems):
    own = lax.axis_index("col") % 2 * (TOTAL // 2)
    away = (TOTAL // 2) - own
    keep_left = pltpu.make_async_copy(left_m, kept.at[:LEFT_ROWS, :], sems.at[0])
    keep_right = pltpu.make_async_copy(right_m, kept.at[LEFT_ROWS:KEPT_ROWS, :], sems.at[1])
    by_col = order(BY_COL)
    unpack(dot(by_col, both_w[:, :WIRE]), left_m, 0)
    keep_left.start()
    unpack(dot(by_col, both_w[:, WIRE:]), right_m, pl.multiple_of(own, 32))
    unpack(dot(by_col, other_w[...]), right_m, pl.multiple_of(away, 32))
    keep_right.start()
    mixed = dot(left_m[...], right_m[...], LAST).astype(BF16)
    pack(dot(mixed, spread[...]), packed)
    wire[...] = move(BY_ROW, packed[...].astype(BF16)).astype(BF16)
    keep_left.wait()
    keep_right.wait()


def turn_kernel(mixed_w, saved, wire, mixed_s, d_mixed_s, d_hat, sem):
    fetch = pltpu.make_async_copy(saved.at[D_HAT:SAVED, :], d_hat, sem)
    fetch.start()
    mixed_s[...] = move(BY_HALF, mixed_w[...])
    fetch.wait()

    @pl.loop(0, STEPS)
    def _(step):
        rows, cols = place_of(step)
        hat, scale = normalise(mixed_s[rows, cols])
        d_mixed_s[rows, cols] = normalise_back(d_hat[:, lanes_of(step)], hat, scale).astype(BF16)

    wire[...] = move(BY_CHANNEL, d_mixed_s[...]).astype(BF16)


def update_kernel(
    mixed_w, saved, weight, gain, shift, out_gain, out_shift, out_weight, out_bias,
    update, grad_out, grad_gate, d_normed,
    padded, mixed_s, held, sem,
):
    fetch = pltpu.make_async_copy(saved.at[HAT:D_HAT, :], held, sem)
    fetch.start()
    mixed_s[...] = move(BY_HALF, mixed_w[...])
    gain_c, shift_c = column(gain), column(shift)
    out_gain_c, out_shift_c, out_bias_c = column(out_gain), column(out_shift), column(out_bias)
    out_t = split(out_weight[...].T)
    gate_w = split(weight[:, 4 * WIDTH :])
    grad_out[...] = jnp.zeros_like(grad_out)
    grad_gate[...] = jnp.zeros_like(grad_gate)
    fetch.wait()

    @pl.loop(0, STEPS)
    def _(step):
        lanes = lanes_of(step)
        rows, cols = place_of(step)
        hat_m, _ = normalise(mixed_s[rows, cols])
        normed = split(hat_m * out_gain_c + out_shift_c)
        result = fine(out_t, normed) + out_bias_c
        is_open = held[OPEN - HAT : GIVEN - HAT, lanes]
        padded[lanes, :] = (is_open * result).T
        given = held[GIVEN - HAT :, lanes]
        grad_out[...] += fine(normed, split(given), LAST)
        d_gate = split(given * result * (1.0 - is_open))
        grad_gate[...] += fine(
            split(held[: OPEN - HAT, lanes] * gain_c + shift_c), d_gate, LAST
        )
        d_normed[:, lanes] = fine(gate_w, d_gate)

    drain(update, padded)


def unmix_right_kernel(
    d_w, kept, spread,
    d_mixed, own_wire, away_wire,
    d_mixed_m, terms, packed, left_m, sem,
):
    own = lax.axis_index("col") % 2 * (TOTAL // 2)
    away = (TOTAL // 2) - own
    get_left = pltpu.make_async_copy(kept.at[:LEFT_ROWS, :], left_m, sem)
    get_left.start()
    by_row = order(BY_ROW)
    unpack(move(BY_COL, d_w[...]), d_mixed_m, 0)
    d_mixed[...] = dot(d_mixed_m[...], spread[...], LAST).astype(BF16)
    get_left.wait()
    terms[...] = dot(d_mixed[...], left_m[...], ((0,), (0,)))
    pack(terms[pl.ds(pl.multiple_of(away, 32), TOTAL // 2), :], packed)
    away_wire[...] = dot(by_row, packed[...].astype(BF16)).astype(BF16)
    pack(terms[pl.ds(pl.multiple_of(own, 32), TOTAL // 2), :], packed)
    own_wire[...] = dot(by_row, packed[...].astype(BF16)).astype(BF16)


def unmix_left_kernel(d_mixed, kept, left_wire, packed, right_m, sem):
    get_right = pltpu.make_async_copy(kept.at[LEFT_ROWS:KEPT_ROWS, :], right_m, sem)
    get_right.start()
    by_row = order(BY_ROW)
    get_right.wait()
    pack(dot(d_mixed[...], right_m[...]), packed)
    left_wire[...] = dot(by_row, packed[...].astype(BF16)).astype(BF16)


def d_hidden_of(d_left_s, d_right_s, factors, step):
    rows, cols = place_of(step)
    lanes = lanes_of(step)
    parts = []
    for i, ref in enumerate((d_left_s, d_right_s)):
        given = ref[rows, cols]
        for j in range(2):
            start = (2 * i + j) * WIDTH
            parts.append(given * factors[start : start + WIDTH, lanes])
    return split(jnp.concatenate(parts, axis=0))


def fetch_saved(saved, held, sems, step):
    lanes = lanes_of(step)
    return pltpu.make_async_copy(saved.at[:OPEN, lanes], held.at[:, lanes], sems.at[step])


def weight_kernel(
    both_w, saved, gain, shift, grad_gate, grad_out,
    grads,
    d_left_s, d_right_s, total, held, sems,
):
    for step in range(STEPS):
        fetch_saved(saved, held, sems, step).start()
    by_half = order(BY_HALF)
    d_left_s[...] = dot(by_half, both_w[:, :WIRE])
    d_right_s[...] = dot(by_half, both_w[:, WIRE:])
    gain_c, shift_c = column(gain), column(shift)
    total[...] = jnp.zeros_like(total)

    @pl.loop(0, STEPS)
    def _(step):
        fetch_saved(saved, held, sems, step).wait()
        d_hidden = d_hidden_of(d_left_s, d_right_s, held, step)
        normed = split(held[HAT:OPEN, lanes_of(step)] * gain_c + shift_c)
        total[...] += fine(normed, d_hidden, LAST)

    grads[:WIDTH, :] = total[:, : 3 * WIDTH]
    grads[WIDTH:, :WIDTH] = total[:, 3 * WIDTH :]
    grads[WIDTH:, WIDTH : 2 * WIDTH] = grad_gate[...]
    grads[WIDTH:, 2 * WIDTH :] = grad_out[...]


def pair_kernel(
    both_w, saved, scale, d_normed, weight, gain,
    grad_pair,
    d_left_s, d_right_s, padded, held, sems,
):
    for step in range(STEPS):
        fetch_saved(saved, held, sems, step).start()
    by_half = order(BY_HALF)
    d_left_s[...] = dot(by_half, both_w[:, :WIRE])
    d_right_s[...] = dot(by_half, both_w[:, WIRE:])
    gain_c = column(gain)
    weight_s = split(weight[:, : 4 * WIDTH])

    @pl.loop(0, STEPS)
    def _(step):
        fetch_saved(saved, held, sems, step).wait()
        lanes = lanes_of(step)
        d_hidden = d_hidden_of(d_left_s, d_right_s, held, step)
        d_hat = (fine(weight_s, d_hidden) + d_normed[:, lanes]) * gain_c
        padded[lanes, :] = normalise_back(d_hat, held[HAT:OPEN, lanes], scale[:, lanes]).T

    drain(grad_pair, padded)


def join_kernel(own, other, grad_proj, grad_out):
    first = lax.axis_index("col") % 2 == 0
    own, other = own[...].astype(F32), other[...].astype(F32)
    upper, lower = jnp.where(first, own, other), jnp.where(first, other, own)
    grad_proj[:, : 3 * WIDTH] = upper
    grad_proj[:, 3 * WIDTH :] = lower[:, : 2 * WIDTH]
    grad_out[...] = lower[:, 2 * WIDTH :]


class Raw:
    def __init__(self, value):
        self.value = value


def call(kernel, outs, scratch, *args, smem=0, work=2e9, room=48):
    operands = [a.value if isinstance(a, Raw) else a for a in args]
    results = [jax.ShapeDtypeStruct(*(o.value if isinstance(o, Raw) else o)) for o in outs]

    def spec(value, raw):
        if raw:
            return pl.BlockSpec(memory_space=pl.ANY)
        return pl.BlockSpec(value.shape, lambda i: (0,) * len(value.shape))

    specs = [spec(v, isinstance(w, Raw)) for v, w in zip([*operands, *results], [*args, *outs])]
    specs[:smem] = [pl.BlockSpec(memory_space=pltpu.SMEM)] * smem
    return pl.pallas_call(
        kernel,
        grid=(1,),
        out_shape=results,
        in_specs=specs[: len(args)],
        out_specs=specs[len(args) :],
        scratch_shapes=[pltpu.VMEM(*s) if isinstance(s, tuple) else s for s in scratch],
        compiler_params=pltpu.CompilerParams(vmem_limit_bytes=room * 2**20),
        cost_estimate=pl.CostEstimate(flops=int(work), bytes_accessed=4 * 2**20, transcendentals=0),
    )(*operands)


def spin(step, count, inner):
    size = 32 if inner != 2 else 8
    return [
        (i, i - (i // inner % count) * inner + ((i // inner + step) % count) * inner)
        for i in range(size)
    ]


LINES = [
    [(y * 8 + high * 4 + x) * COL_N + low * 2 + core for high in range(2) for low in range(4)]
    for y in range(4)
    for x in range(4)
    for core in range(2)
]


def meet(value, axis, count, inner):
    others = [lax.ppermute(value, axis, spin(k, count, inner)) for k in range(1, count)]
    if count == 2:
        return value + others[0]
    one, two, three = others
    return (value + two) + (one + three)


def sum_over_devices(grads, row, col, beside):
    core, x = col % 2, row % 4
    pick = lambda a, i: lax.dynamic_index_in_dim(a, i, 0, keepdims=False)
    pairs = grads.reshape(2, WIDTH, 3 * WIDTH)
    taken = lax.ppermute(pick(pairs, 1 - core), "col", SWAP)
    total = pick(pairs, core) + taken
    total = total.reshape(4, WIDTH // 4, 3 * WIDTH)
    taken = [
        lax.ppermute(pick(total, (x + k) % 4), "row", spin(k, 4, 1)) for k in (1, 2, 3)
    ]
    total = (pick(total, x) + taken[0]) + (taken[1] + taken[2])
    total = meet(total, "row", 4, 8)
    total = jnp.broadcast_to(total.astype(BF16)[None], (8,) + total.shape)
    total = lax.all_to_all(total, BOTH, 0, 0, axis_index_groups=LINES, tiled=True)
    total = jnp.sum(total.astype(F32), axis=0).astype(BF16)
    total, beside = lax.optimization_barrier((total, beside))
    parts = jnp.zeros((4, WIDTH // 4, 3 * WIDTH), BF16)
    parts = lax.dynamic_update_index_in_dim(parts, total, x, 0)
    for k in (1, 2, 3):
        taken = lax.ppermute(total, "row", spin(k, 4, 1))
        parts = lax.dynamic_update_index_in_dim(parts, taken, (x + 4 - k) % 4, 0)
    parts = parts.reshape(WIDTH, 3 * WIDTH)
    other = lax.ppermute(parts, "col", SWAP)
    return parts, other, beside


def exchange(chunks):
    return lax.all_to_all(chunks, BOTH, 0, 0, tiled=True)


def shards(
    pair,
    cotangent,
    residue_mask,
    ln_gain,
    ln_bias,
    proj_weight,
    proj_bias,
    norm_gain,
    norm_bias,
    out_weight,
    out_bias,
):
    spread = spread_table()
    shape = pair.shape
    places = ROWS * COLS
    row, col = lax.axis_index("row"), lax.axis_index("col")
    pair = pair.reshape(places, WIDTH)
    cotangent = cotangent.reshape(places, WIDTH)
    line = lambda v: v.reshape(-1, WIDTH)
    gain, shift, bias = line(ln_gain), line(ln_bias), line(proj_bias)
    out_gain, out_shift, out_bias = line(norm_gain), line(norm_bias), line(out_bias)
    whole = ((LANES, WIDTH), F32)
    turned = ((WIDTH, LANES), F32)
    square = ((WIDTH, WIDTH), F32)
    halves = lambda kind: ((DEVICES, WIRE), kind)

    wire, mask = call(
        project_kernel,
        [((DEVICES, LANES), BF16), ((1, LANES), F32)],
        [whole, halves(BF16), halves(BF16)],
        residue_mask, pair, proj_weight, bias, gain, shift,
        smem=1,
        room=62,
    )
    got = exchange(wire.reshape(DEVICES, 2, WIRE)).reshape(DEVICES, LANES)
    dma = pltpu.SemaphoreType.DMA
    scale, saved = call(
        prepare_kernel,
        [((1, LANES), F32), Raw(((SAVED, LANES), F32))],
        [whole, whole, ((SAVED, LANES), F32), dma((STEPS,))],
        mask, pair, cotangent, proj_weight, bias, gain, shift, out_gain, out_weight,
        work=1e10,
    )
    other_w = lax.ppermute(got[:, WIRE:], "col", SWAP)
    left_s, right_s = ((LEFT_ROWS, COL_N * 128), BF16), ((TOTAL, COL_N * 128), BF16)
    wire, kept = call(
        mix_kernel,
        [halves(BF16), Raw(((KEPT, COL_N * 128), BF16))],
        [left_s, right_s, halves(F32), dma((2,))],
        got, other_w, spread,
    )
    mixed_w = exchange(wire.reshape(DEVICES, 2, WIRE // 2)).reshape(DEVICES, WIRE)
    (wire,) = call(
        turn_kernel,
        [halves(BF16)],
        [halves(F32), halves(BF16), turned, dma],
        mixed_w, Raw(saved),
    )
    got = exchange(wire.reshape(DEVICES, 2, WIRE // 2)).reshape(DEVICES, WIRE)
    update, grad_out, grad_gate, d_normed = call(
        update_kernel,
        [((places, WIDTH), F32), square, square, turned],
        [whole, halves(F32), ((D_HAT - HAT, LANES), F32), dma],
        mixed_w, Raw(saved), proj_weight, gain, shift, out_gain, out_shift, out_weight, out_bias,
        work=8e9,
    )
    d_mixed, own_wire, away_wire = call(
        unmix_right_kernel,
        [((LEFT_ROWS, TOTAL), BF16), halves(BF16), halves(BF16)],
        [left_s, ((TOTAL, COL_N * 128), F32), halves(F32), left_s, dma],
        got, Raw(kept), spread,
    )
    other_wire = lax.ppermute(away_wire, "col", SWAP)
    (left_wire,) = call(
        unmix_left_kernel,
        [halves(BF16)],
        [halves(F32), right_s, dma],
        d_mixed, Raw(kept),
    )
    right_wire = (own_wire.astype(F32) + other_wire.astype(F32)).astype(BF16)
    got = exchange(jnp.stack([left_wire, right_wire], axis=1)).reshape(DEVICES, LANES)
    held = ((OPEN, LANES), F32)
    (grads,) = call(
        weight_kernel,
        [((DEVICES, 3 * WIDTH), F32)],
        [halves(F32), halves(F32), ((WIDTH, 4 * WIDTH), F32), held, dma((STEPS,))],
        got, Raw(saved), gain, shift, grad_gate, grad_out,
    )
    (grad_pair,) = call(
        pair_kernel,
        [((places, WIDTH), F32)],
        [halves(F32), halves(F32), whole, held, dma((STEPS,))],
        got, Raw(saved), scale, d_normed, proj_weight, gain,
        work=8e9,
    )
    own, other, grad_pair = sum_over_devices(grads, row, col, grad_pair)
    grad_proj, grad_out = call(
        join_kernel, [((WIDTH, 5 * WIDTH), F32), square], [], own, other, work=1e8
    )
    return update.reshape(shape), grad_pair.reshape(shape), grad_proj, grad_out


def solution(mesh):
    in_specs = (P("row", "col", None), P("row", "col", None)) + (P(),) * 9
    out_specs = (P("row", "col", None), P("row", "col", None), P(), P())
    return jax.shard_map(shards, mesh=mesh, in_specs=in_specs, out_specs=out_specs, check_vma=False)
```

```python
import jax
import jax.numpy as jnp
import numpy as np
from jax import lax
from jax.experimental import pallas as pl
from jax.experimental.pallas import tpu as pltpu
from jax.sharding import PartitionSpec as P

BOTH = ("row", "col")
SWAP = [(0, 1), (1, 0), (2, 3), (3, 2), (4, 5), (5, 4), (6, 7), (7, 6)]
ROWS, COLS, WIDTH = 18, 72, 128
ROW_N, COL_N = 32, 8
DEVICES = ROW_N * COL_N
HALF = ROWS // 2
PIECE = HALF * COLS
WIRE = 768
LANES = 2 * WIRE
TOTAL = ROW_N * ROWS
GROUP = ROW_N // COL_N
STEP = 768
STEPS = LANES // STEP
F32, BF16 = jnp.float32, jnp.bfloat16


def one_hot(targets, length):
    table = np.zeros((len(targets), length), np.float32)
    table[np.arange(len(targets)), targets] = 1
    return jnp.asarray(table, BF16)


def spread_table():
    place, row = np.divmod(np.arange(TOTAL), ROW_N)
    col, part = np.divmod(row, GROUP)
    return one_hot(col * 128 + part * ROWS + place, COL_N * 128)


HAT, OPEN, GIVEN, D_HAT, SAVED = 512, 640, 768, 896, 1024
LEFT_ROWS, KEPT_ROWS, KEPT = 288, 864, 3072
BY_COL, BY_ROW, BY_HALF, BY_CHANNEL = 5, 3, 7, 1


def order(bits):
    n = lax.broadcasted_iota(jnp.int32, (DEVICES, DEVICES), 0)
    target = ((n & ((1 << bits) - 1)) << (8 - bits)) + (n >> bits)
    other = lax.broadcasted_iota(jnp.int32, (DEVICES, DEVICES), 1)
    return jnp.where(other == target, 1.0, 0.0).astype(BF16)


PLAIN = ((1,), (0,))
LAST = ((1,), (1,))


def dot(a, b, contract=PLAIN):
    return lax.dot_general(a, b, (contract, ((), ())), preferred_element_type=F32)


def split(x):
    high = x.astype(BF16)
    return high, (x - high.astype(F32)).astype(BF16)


def fine(a, b, contract=PLAIN):
    return dot(a[0], b[0], contract) + (dot(a[0], b[1], contract) + dot(a[1], b[0], contract))


def move(bits, values):
    return dot(order(bits), values)


def sigmoid(x):
    return 0.5 * jnp.tanh(0.5 * x) + 0.5


def normalise(values):
    centred = values - jnp.mean(values, axis=0, keepdims=True)
    spread = jnp.mean(centred * centred, axis=0, keepdims=True)
    scale = lax.rsqrt(spread + 1e-05)
    return centred * scale, scale


def normalise_back(d_hat, hat, scale):
    return scale * (
        d_hat
        - jnp.mean(d_hat, axis=0, keepdims=True)
        - hat * jnp.mean(d_hat * hat, axis=0, keepdims=True)
    )


def column(ref):
    return jnp.broadcast_to(ref[...], (8, WIDTH)).T[:, :1]


def columns(ref):
    table = jnp.concatenate([ref[...], jnp.zeros((3, WIDTH), F32)], axis=0).T
    return [table[:, i : i + 1] for i in range(5)]


def fill(padded, block):
    for half in range(2):
        padded[pl.ds(half * WIRE, PIECE), :] = block[pl.ds(half * PIECE, PIECE), :]
        padded[pl.ds(half * WIRE + PIECE, WIRE - PIECE), :] = jnp.zeros(
            (WIRE - PIECE, WIDTH), F32
        )


def drain(block, padded):
    for half in range(2):
        block[pl.ds(half * PIECE, PIECE), :] = padded[pl.ds(half * WIRE, PIECE), :]


def place_of(step):
    per = WIRE // STEP
    half = step // per
    return (
        pl.ds(pl.multiple_of(half * WIDTH, WIDTH), WIDTH),
        pl.ds(pl.multiple_of((step - half * per) * STEP, STEP), STEP),
    )


def lanes_of(step):
    return pl.ds(pl.multiple_of(step * STEP, STEP), STEP)


def build_mask(row, col, valid, mask):
    lane = lax.broadcasted_iota(jnp.int32, (8, 128), 1)
    cols = jnp.zeros((8, 128), F32)
    for k in range(COLS):
        cols = jnp.where(lane == k, valid[col * COLS + k].astype(F32), cols)
    cols = jnp.concatenate([cols, jnp.zeros((8, WIRE - 128), F32)], axis=1)
    shifted = [cols] + [pltpu.roll(cols, i * COLS, 1) for i in range(1, HALF)]
    for half in range(2):
        total = jnp.zeros((8, WIRE), F32)
        for i in range(HALF):
            total = total + valid[row * ROWS + half * HALF + i].astype(F32) * shifted[i]
        mask[:, half * WIRE : (half + 1) * WIRE] = total[:1]


def project_kernel(
    valid, pair, weight, bias, gain, shift,
    wire, mask,
    padded, by_channel, held, sems,
):
    build_mask(lax.axis_index("row"), lax.axis_index("col"), valid, mask)
    fill(padded, pair)
    gain_c, shift_c = column(gain), column(shift)
    bias_c = jnp.concatenate(columns(bias)[:4], axis=0)
    weight_t = split(weight[:, : 4 * WIDTH].T)
    by_channel[...] = order(BY_CHANNEL)

    def leave(step, side):
        lanes = pl.ds(pl.multiple_of(side * WIRE + step * STEP, STEP), STEP)
        pieces = held.at[:, lanes], wire.at[:, lanes]
        return lanes, pltpu.make_async_copy(*pieces, sems.at[2 * step + side])

    @pl.loop(0, WIRE // STEP)
    def _(step):
        sides = [], []
        for half in range(2):
            lanes = pl.ds(pl.multiple_of(half * WIRE + step * STEP, STEP), STEP)
            hat, _ = normalise(padded[lanes, :].T)
            hidden = fine(weight_t, split(hat * gain_c + shift_c)) + bias_c
            valid = mask[:, lanes]
            for side in range(2):
                value = hidden[2 * side * WIDTH : (2 * side + 1) * WIDTH]
                opened = sigmoid(hidden[(2 * side + 1) * WIDTH : (2 * side + 2) * WIDTH])
                sides[side].append((valid * opened * value).astype(BF16))
        for side in range(2):
            lanes, copy = leave(step, side)
            both = jnp.concatenate(sides[side], axis=0)
            held[:, lanes] = dot(by_channel[...], both).astype(BF16)
            copy.start()

    @pl.loop(0, WIRE // STEP)
    def _(step):
        for side in range(2):
            leave(step, side)[1].wait()


def prepare_kernel(
    mask, pair, cotangent, weight, bias, gain, shift, out_gain, out_weight,
    scale_o, saved,
    padded, padded_c, held, sems,
):
    fill(padded, pair)
    fill(padded_c, cotangent)
    gain_c, shift_c, out_gain_c = column(gain), column(shift), column(out_gain)
    bias_c = jnp.concatenate(columns(bias), axis=0)
    weight_t = split(weight[...].T)
    out_w = split(out_weight[...])

    def leave(step):
        lanes = lanes_of(step)
        return pltpu.make_async_copy(held.at[:, lanes], saved.at[:, lanes], sems.at[step])

    @pl.loop(0, STEPS)
    def _(step):
        lanes = lanes_of(step)
        hat, scale = normalise(padded[lanes, :].T)
        held[HAT:OPEN, lanes] = hat
        scale_o[:, lanes] = scale
        hidden = fine(weight_t, split(hat * gain_c + shift_c)) + bias_c
        valid = mask[:, lanes]
        for i in range(2):
            opened = sigmoid(hidden[(2 * i + 1) * WIDTH : (2 * i + 2) * WIDTH])
            factor = valid * opened
            held[2 * i * WIDTH : (2 * i + 1) * WIDTH, lanes] = factor
            held[(2 * i + 1) * WIDTH : (2 * i + 2) * WIDTH, lanes] = (
                factor * (1.0 - opened) * hidden[2 * i * WIDTH : (2 * i + 1) * WIDTH]
            )
        opened = sigmoid(hidden[4 * WIDTH :])
        held[OPEN:GIVEN, lanes] = opened
        d_result = padded_c[lanes, :].T * opened
        held[GIVEN:D_HAT, lanes] = d_result
        held[D_HAT:SAVED, lanes] = fine(out_w, split(d_result)) * out_gain_c
        leave(step).start()

    @pl.loop(0, STEPS)
    def _(step):
        leave(step).wait()


def unpack(values, out, base):
    keep = lax.broadcasted_iota(jnp.int32, (DEVICES, 128), 1) < COLS
    for i in range(HALF):
        tile, offset = divmod(i * COLS, 128)
        part = values[:, tile * 128 : tile * 128 + 256]
        if offset:
            part = pltpu.roll(part, 256 - offset, 1)
        part = jnp.where(keep, part[:, :128], 0.0).astype(BF16)
        for q in range(COL_N):
            out[pl.ds(base + i * ROW_N, ROW_N), q * 128 : (q + 1) * 128] = part[
                q * ROW_N : (q + 1) * ROW_N
            ]


def pack(values, out):
    out[...] = jnp.zeros_like(out)
    for i in range(HALF):
        tile, offset = divmod(i * COLS, 128)
        part = jnp.concatenate(
            [
                values[i * ROW_N : (i + 1) * ROW_N, q * 128 : (q + 1) * 128]
                for q in range(COL_N)
            ],
            axis=0,
        )
        part = jnp.concatenate([part, jnp.zeros_like(part)], axis=1)
        if offset:
            part = pltpu.roll(part, offset, 1)
        out[:, tile * 128 : tile * 128 + 256] += part


def mix_kernel(both_w, other_w, spread, wire, kept, left_m, right_m, packed, sems):
    own = lax.axis_index("col") % 2 * (TOTAL // 2)
    away = (TOTAL // 2) - own
    keep_left = pltpu.make_async_copy(left_m, kept.at[:LEFT_ROWS, :], sems.at[0])
    keep_right = pltpu.make_async_copy(right_m, kept.at[LEFT_ROWS:KEPT_ROWS, :], sems.at[1])
    by_col = order(BY_COL)
    unpack(dot(by_col, both_w[:, :WIRE]), left_m, 0)
    keep_left.start()
    unpack(dot(by_col, both_w[:, WIRE:]), right_m, pl.multiple_of(own, 32))
    unpack(dot(by_col, other_w[...]), right_m, pl.multiple_of(away, 32))
    keep_right.start()
    mixed = dot(left_m[...], right_m[...], LAST).astype(BF16)
    pack(dot(mixed, spread[...]), packed)
    wire[...] = move(BY_ROW, packed[...].astype(BF16)).astype(BF16)
    keep_left.wait()
    keep_right.wait()


def turn_kernel(mixed_w, saved, wire, mixed_s, d_mixed_s, d_hat, sems):
    def fetch(step):
        lanes = lanes_of(step)
        pieces = saved.at[D_HAT:SAVED, lanes], d_hat.at[:, lanes]
        return pltpu.make_async_copy(*pieces, sems.at[step])

    for step in range(STEPS):
        fetch(step).start()
    mixed_s[...] = move(BY_HALF, mixed_w[...])

    @pl.loop(0, STEPS)
    def _(step):
        rows, cols = place_of(step)
        hat, scale = normalise(mixed_s[rows, cols])
        fetch(step).wait()
        d_mixed_s[rows, cols] = normalise_back(d_hat[:, lanes_of(step)], hat, scale).astype(BF16)

    wire[...] = move(BY_CHANNEL, d_mixed_s[...]).astype(BF16)


def update_kernel(
    mixed_w, saved, weight, gain, shift, out_gain, out_shift, out_weight, out_bias,
    update, grad_out, grad_gate, d_normed,
    padded, mixed_s, held, sem,
):
    fetch = pltpu.make_async_copy(saved.at[HAT:D_HAT, :], held, sem)
    fetch.start()
    mixed_s[...] = move(BY_HALF, mixed_w[...])
    gain_c, shift_c = column(gain), column(shift)
    out_gain_c, out_shift_c, out_bias_c = column(out_gain), column(out_shift), column(out_bias)
    out_t = split(out_weight[...].T)
    gate_w = split(weight[:, 4 * WIDTH :])
    grad_out[...] = jnp.zeros_like(grad_out)
    grad_gate[...] = jnp.zeros_like(grad_gate)
    fetch.wait()

    @pl.loop(0, STEPS)
    def _(step):
        lanes = lanes_of(step)
        rows, cols = place_of(step)
        hat_m, _ = normalise(mixed_s[rows, cols])
        normed = split(hat_m * out_gain_c + out_shift_c)
        result = fine(out_t, normed) + out_bias_c
        is_open = held[OPEN - HAT : GIVEN - HAT, lanes]
        padded[lanes, :] = (is_open * result).T
        given = held[GIVEN - HAT :, lanes]
        grad_out[...] += fine(normed, split(given), LAST)
        d_gate = split(given * result * (1.0 - is_open))
        grad_gate[...] += fine(
            split(held[: OPEN - HAT, lanes] * gain_c + shift_c), d_gate, LAST
        )
        d_normed[:, lanes] = fine(gate_w, d_gate)

    drain(update, padded)


def unmix_right_kernel(
    d_w, kept, spread,
    d_mixed, own_wire, away_wire,
    d_mixed_m, terms, packed, left_m, sem,
):
    own = lax.axis_index("col") % 2 * (TOTAL // 2)
    away = (TOTAL // 2) - own
    get_left = pltpu.make_async_copy(kept.at[:LEFT_ROWS, :], left_m, sem)
    get_left.start()
    by_row = order(BY_ROW)
    unpack(move(BY_COL, d_w[...]), d_mixed_m, 0)
    d_mixed[...] = dot(d_mixed_m[...], spread[...], LAST).astype(BF16)
    get_left.wait()
    terms[...] = dot(d_mixed[...], left_m[...], ((0,), (0,)))
    pack(terms[pl.ds(pl.multiple_of(away, 32), TOTAL // 2), :], packed)
    away_wire[...] = dot(by_row, packed[...].astype(BF16)).astype(BF16)
    pack(terms[pl.ds(pl.multiple_of(own, 32), TOTAL // 2), :], packed)
    own_wire[...] = dot(by_row, packed[...].astype(BF16)).astype(BF16)


def unmix_left_kernel(d_mixed, kept, left_wire, packed, right_m, sem):
    get_right = pltpu.make_async_copy(kept.at[LEFT_ROWS:KEPT_ROWS, :], right_m, sem)
    get_right.start()
    by_row = order(BY_ROW)
    get_right.wait()
    pack(dot(d_mixed[...], right_m[...]), packed)
    left_wire[...] = dot(by_row, packed[...].astype(BF16)).astype(BF16)


def d_hidden_of(d_left_s, d_right_s, factors, step):
    rows, cols = place_of(step)
    lanes = lanes_of(step)
    parts = []
    for i, ref in enumerate((d_left_s, d_right_s)):
        given = ref[rows, cols]
        for j in range(2):
            start = (2 * i + j) * WIDTH
            parts.append(given * factors[start : start + WIDTH, lanes])
    return split(jnp.concatenate(parts, axis=0))


def fetch_saved(saved, held, sems, step):
    lanes = lanes_of(step)
    return pltpu.make_async_copy(saved.at[:OPEN, lanes], held.at[:, lanes], sems.at[step])


def weight_kernel(
    both_w, saved, gain, shift, grad_gate, grad_out,
    grads,
    d_left_s, d_right_s, total, held, sems,
):
    for step in range(STEPS):
        fetch_saved(saved, held, sems, step).start()
    by_half = order(BY_HALF)
    d_left_s[...] = dot(by_half, both_w[:, :WIRE])
    d_right_s[...] = dot(by_half, both_w[:, WIRE:])
    gain_c, shift_c = column(gain), column(shift)
    total[...] = jnp.zeros_like(total)

    @pl.loop(0, STEPS)
    def _(step):
        fetch_saved(saved, held, sems, step).wait()
        d_hidden = d_hidden_of(d_left_s, d_right_s, held, step)
        normed = split(held[HAT:OPEN, lanes_of(step)] * gain_c + shift_c)
        total[...] += fine(normed, d_hidden, LAST)

    grads[:WIDTH, :] = total[:, : 3 * WIDTH]
    grads[WIDTH:, :WIDTH] = total[:, 3 * WIDTH :]
    grads[WIDTH:, WIDTH : 2 * WIDTH] = grad_gate[...]
    grads[WIDTH:, 2 * WIDTH :] = grad_out[...]


def pair_kernel(
    both_w, saved, scale, d_normed, weight, gain,
    grad_pair,
    d_left_s, d_right_s, padded, held, sems,
):
    for step in range(STEPS):
        fetch_saved(saved, held, sems, step).start()
    by_half = order(BY_HALF)
    d_left_s[...] = dot(by_half, both_w[:, :WIRE])
    d_right_s[...] = dot(by_half, both_w[:, WIRE:])
    gain_c = column(gain)
    weight_s = split(weight[:, : 4 * WIDTH])

    @pl.loop(0, STEPS)
    def _(step):
        fetch_saved(saved, held, sems, step).wait()
        lanes = lanes_of(step)
        d_hidden = d_hidden_of(d_left_s, d_right_s, held, step)
        d_hat = (fine(weight_s, d_hidden) + d_normed[:, lanes]) * gain_c
        padded[lanes, :] = normalise_back(d_hat, held[HAT:OPEN, lanes], scale[:, lanes]).T

    drain(grad_pair, padded)


def join_kernel(own, other, grad_proj, grad_out):
    first = lax.axis_index("col") % 2 == 0
    own, other = own[...].astype(F32), other[...].astype(F32)
    upper, lower = jnp.where(first, own, other), jnp.where(first, other, own)
    grad_proj[:, : 3 * WIDTH] = upper
    grad_proj[:, 3 * WIDTH :] = lower[:, : 2 * WIDTH]
    grad_out[...] = lower[:, 2 * WIDTH :]


class Raw:
    def __init__(self, value):
        self.value = value


def call(kernel, outs, scratch, *args, smem=0, work=2e9, room=48):
    operands = [a.value if isinstance(a, Raw) else a for a in args]
    results = [jax.ShapeDtypeStruct(*(o.value if isinstance(o, Raw) else o)) for o in outs]

    def spec(value, raw):
        if raw:
            return pl.BlockSpec(memory_space=pl.ANY)
        return pl.BlockSpec(value.shape, lambda i: (0,) * len(value.shape))

    specs = [spec(v, isinstance(w, Raw)) for v, w in zip([*operands, *results], [*args, *outs])]
    specs[:smem] = [pl.BlockSpec(memory_space=pltpu.SMEM)] * smem
    return pl.pallas_call(
        kernel,
        grid=(1,),
        out_shape=results,
        in_specs=specs[: len(args)],
        out_specs=specs[len(args) :],
        scratch_shapes=[pltpu.VMEM(*s) if isinstance(s, tuple) else s for s in scratch],
        compiler_params=pltpu.CompilerParams(vmem_limit_bytes=room * 2**20),
        cost_estimate=pl.CostEstimate(flops=int(work), bytes_accessed=4 * 2**20, transcendentals=0),
    )(*operands)


def spin(step, count, inner):
    size = 32 if inner != 2 else 8
    return [
        (i, i - (i // inner % count) * inner + ((i // inner + step) % count) * inner)
        for i in range(size)
    ]


LINES = [
    [(y * 8 + high * 4 + x) * COL_N + low * 2 + core for high in range(2) for low in range(4)]
    for y in range(4)
    for x in range(4)
    for core in range(2)
]


def meet(value, axis, count, inner):
    others = [lax.ppermute(value, axis, spin(k, count, inner)) for k in range(1, count)]
    if count == 2:
        return value + others[0]
    one, two, three = others
    return (value + two) + (one + three)


def sum_over_devices(grads, row, col, beside):
    core, x = col % 2, row % 4
    pick = lambda a, i: lax.dynamic_index_in_dim(a, i, 0, keepdims=False)
    pairs = grads.reshape(2, WIDTH, 3 * WIDTH)
    taken = lax.ppermute(pick(pairs, 1 - core), "col", SWAP)
    total = pick(pairs, core) + taken
    total = total.reshape(4, WIDTH // 4, 3 * WIDTH)
    taken = [
        lax.ppermute(pick(total, (x + k) % 4), "row", spin(k, 4, 1)) for k in (1, 2, 3)
    ]
    total = (pick(total, x) + taken[0]) + (taken[1] + taken[2])
    total = meet(total, "row", 4, 8)
    total = jnp.broadcast_to(total.astype(BF16)[None], (8,) + total.shape)
    total = lax.all_to_all(total, BOTH, 0, 0, axis_index_groups=LINES, tiled=True)
    total = jnp.sum(total.astype(F32), axis=0).astype(BF16)
    total, beside = lax.optimization_barrier((total, beside))
    parts = jnp.zeros((4, WIDTH // 4, 3 * WIDTH), BF16)
    parts = lax.dynamic_update_index_in_dim(parts, total, x, 0)
    for k in (1, 2, 3):
        taken = lax.ppermute(total, "row", spin(k, 4, 1))
        parts = lax.dynamic_update_index_in_dim(parts, taken, (x + 4 - k) % 4, 0)
    parts = parts.reshape(WIDTH, 3 * WIDTH)
    other = lax.ppermute(parts, "col", SWAP)
    return parts, other, beside


def exchange(chunks):
    return lax.all_to_all(chunks, BOTH, 0, 0, tiled=True)


def shards(
    pair,
    cotangent,
    residue_mask,
    ln_gain,
    ln_bias,
    proj_weight,
    proj_bias,
    norm_gain,
    norm_bias,
    out_weight,
    out_bias,
):
    spread = spread_table()
    shape = pair.shape
    places = ROWS * COLS
    row, col = lax.axis_index("row"), lax.axis_index("col")
    pair = pair.reshape(places, WIDTH)
    cotangent = cotangent.reshape(places, WIDTH)
    line = lambda v: v.reshape(-1, WIDTH)
    gain, shift, bias = line(ln_gain), line(ln_bias), line(proj_bias)
    out_gain, out_shift, out_bias = line(norm_gain), line(norm_bias), line(out_bias)
    whole = ((LANES, WIDTH), F32)
    turned = ((WIDTH, LANES), F32)
    square = ((WIDTH, WIDTH), F32)
    halves = lambda kind: ((DEVICES, WIRE), kind)

    dma = pltpu.SemaphoreType.DMA
    wire, mask = call(
        project_kernel,
        [Raw(((DEVICES, LANES), BF16)), ((1, LANES), F32)],
        [whole, ((DEVICES, DEVICES), BF16), ((DEVICES, LANES), BF16), dma((STEPS,))],
        residue_mask, pair, proj_weight, bias, gain, shift,
        smem=1,
        room=62,
    )
    got = exchange(wire.reshape(DEVICES, 2, WIRE)).reshape(DEVICES, LANES)
    scale, saved = call(
        prepare_kernel,
        [((1, LANES), F32), Raw(((SAVED, LANES), F32))],
        [whole, whole, ((SAVED, LANES), F32), dma((STEPS,))],
        mask, pair, cotangent, proj_weight, bias, gain, shift, out_gain, out_weight,
        work=1e10,
    )
    other_w = lax.ppermute(got[:, WIRE:], "col", SWAP)
    left_s, right_s = ((LEFT_ROWS, COL_N * 128), BF16), ((TOTAL, COL_N * 128), BF16)
    wire, kept = call(
        mix_kernel,
        [halves(BF16), Raw(((KEPT, COL_N * 128), BF16))],
        [left_s, right_s, halves(F32), dma((2,))],
        got, other_w, spread,
    )
    mixed_w = exchange(wire.reshape(DEVICES, 2, WIRE // 2)).reshape(DEVICES, WIRE)
    (wire,) = call(
        turn_kernel,
        [halves(BF16)],
        [halves(F32), halves(BF16), turned, dma((STEPS,))],
        mixed_w, Raw(saved),
    )
    got = exchange(wire.reshape(DEVICES, 2, WIRE // 2)).reshape(DEVICES, WIRE)
    update, grad_out, grad_gate, d_normed = call(
        update_kernel,
        [((places, WIDTH), F32), square, square, turned],
        [whole, halves(F32), ((D_HAT - HAT, LANES), F32), dma],
        mixed_w, Raw(saved), proj_weight, gain, shift, out_gain, out_shift, out_weight, out_bias,
        work=8e9,
    )
    d_mixed, own_wire, away_wire = call(
        unmix_right_kernel,
        [((LEFT_ROWS, TOTAL), BF16), halves(BF16), halves(BF16)],
        [left_s, ((TOTAL, COL_N * 128), F32), halves(F32), left_s, dma],
        got, Raw(kept), spread,
    )
    other_wire = lax.ppermute(away_wire, "col", SWAP)
    (left_wire,) = call(
        unmix_left_kernel,
        [halves(BF16)],
        [halves(F32), right_s, dma],
        d_mixed, Raw(kept),
    )
    right_wire = (own_wire.astype(F32) + other_wire.astype(F32)).astype(BF16)
    got = exchange(jnp.stack([left_wire, right_wire], axis=1)).reshape(DEVICES, LANES)
    held = ((OPEN, LANES), F32)
    (grads,) = call(
        weight_kernel,
        [((DEVICES, 3 * WIDTH), F32)],
        [halves(F32), halves(F32), ((WIDTH, 4 * WIDTH), F32), held, dma((STEPS,))],
        got, Raw(saved), gain, shift, grad_gate, grad_out,
    )
    (grad_pair,) = call(
        pair_kernel,
        [((places, WIDTH), F32)],
        [halves(F32), halves(F32), whole, held, dma((STEPS,))],
        got, Raw(saved), scale, d_normed, proj_weight, gain,
        work=8e9,
    )
    own, other, grad_pair = sum_over_devices(grads, row, col, grad_pair)
    grad_proj, grad_out = call(
        join_kernel, [((WIDTH, 5 * WIDTH), F32), square], [], own, other, work=1e8
    )
    return update.reshape(shape), grad_pair.reshape(shape), grad_proj, grad_out


def solution(mesh):
    in_specs = (P("row", "col", None), P("row", "col", None)) + (P(),) * 9
    out_specs = (P("row", "col", None), P("row", "col", None), P(), P())
    return jax.shard_map(shards, mesh=mesh, in_specs=in_specs, out_specs=out_specs, check_vma=False)
```

```python
import jax
import jax.numpy as jnp
import numpy as np
from jax import lax
from jax.experimental import pallas as pl
from jax.experimental.pallas import tpu as pltpu
from jax.sharding import PartitionSpec as P

BOTH = ("row", "col")
SWAP = [(0, 1), (1, 0), (2, 3), (3, 2), (4, 5), (5, 4), (6, 7), (7, 6)]
ROWS, COLS, WIDTH = 18, 72, 128
ROW_N, COL_N = 32, 8
DEVICES = ROW_N * COL_N
HALF = ROWS // 2
PIECE = HALF * COLS
WIRE = 768
LANES = 2 * WIRE
TOTAL = ROW_N * ROWS
GROUP = ROW_N // COL_N
STEP = 768
STEPS = LANES // STEP
F32, BF16 = jnp.float32, jnp.bfloat16


def one_hot(targets, length):
    table = np.zeros((len(targets), length), np.float32)
    table[np.arange(len(targets)), targets] = 1
    return jnp.asarray(table, BF16)


def spread_table():
    place, row = np.divmod(np.arange(TOTAL), ROW_N)
    col, part = np.divmod(row, GROUP)
    return one_hot(col * 128 + part * ROWS + place, COL_N * 128)


HAT, OPEN, GIVEN, D_HAT, SAVED = 512, 640, 768, 896, 1024
LEFT_ROWS, KEPT_ROWS, KEPT = 288, 864, 3072
BY_COL, BY_ROW, BY_HALF, BY_CHANNEL = 5, 3, 7, 1


def order(bits):
    n = lax.broadcasted_iota(jnp.int32, (DEVICES, DEVICES), 0)
    target = ((n & ((1 << bits) - 1)) << (8 - bits)) + (n >> bits)
    other = lax.broadcasted_iota(jnp.int32, (DEVICES, DEVICES), 1)
    return jnp.where(other == target, 1.0, 0.0).astype(BF16)


PLAIN = ((1,), (0,))
LAST = ((1,), (1,))


def dot(a, b, contract=PLAIN):
    return lax.dot_general(a, b, (contract, ((), ())), preferred_element_type=F32)


def split(x):
    high = x.astype(BF16)
    return high, (x - high.astype(F32)).astype(BF16)


def fine(a, b, contract=PLAIN):
    return dot(a[0], b[0], contract) + (dot(a[0], b[1], contract) + dot(a[1], b[0], contract))


def move(bits, values):
    return dot(order(bits), values)


def sigmoid(x):
    return 0.5 * jnp.tanh(0.5 * x) + 0.5


def normalise(values):
    centred = values - jnp.mean(values, axis=0, keepdims=True)
    spread = jnp.mean(centred * centred, axis=0, keepdims=True)
    scale = lax.rsqrt(spread + 1e-05)
    return centred * scale, scale


def normalise_back(d_hat, hat, scale):
    return scale * (
        d_hat
        - jnp.mean(d_hat, axis=0, keepdims=True)
        - hat * jnp.mean(d_hat * hat, axis=0, keepdims=True)
    )


def column(ref):
    return jnp.broadcast_to(ref[...], (8, WIDTH)).T[:, :1]


def columns(ref):
    table = jnp.concatenate([ref[...], jnp.zeros((3, WIDTH), F32)], axis=0).T
    return [table[:, i : i + 1] for i in range(5)]


def fill(padded, block):
    for half in range(2):
        padded[pl.ds(half * WIRE, PIECE), :] = block[pl.ds(half * PIECE, PIECE), :]
        padded[pl.ds(half * WIRE + PIECE, WIRE - PIECE), :] = jnp.zeros(
            (WIRE - PIECE, WIDTH), F32
        )


def drain(block, padded):
    for half in range(2):
        block[pl.ds(half * PIECE, PIECE), :] = padded[pl.ds(half * WIRE, PIECE), :]


def place_of(step):
    per = WIRE // STEP
    half = step // per
    return (
        pl.ds(pl.multiple_of(half * WIDTH, WIDTH), WIDTH),
        pl.ds(pl.multiple_of((step - half * per) * STEP, STEP), STEP),
    )


def lanes_of(step):
    return pl.ds(pl.multiple_of(step * STEP, STEP), STEP)


def build_mask(row, col, valid, mask):
    lane = lax.broadcasted_iota(jnp.int32, (8, 128), 1)
    cols = jnp.zeros((8, 128), F32)
    for k in range(COLS):
        cols = jnp.where(lane == k, valid[col * COLS + k].astype(F32), cols)
    cols = jnp.concatenate([cols, jnp.zeros((8, WIRE - 128), F32)], axis=1)
    shifted = [cols] + [pltpu.roll(cols, i * COLS, 1) for i in range(1, HALF)]
    for half in range(2):
        total = jnp.zeros((8, WIRE), F32)
        for i in range(HALF):
            total = total + valid[row * ROWS + half * HALF + i].astype(F32) * shifted[i]
        mask[:, half * WIRE : (half + 1) * WIRE] = total[:1]


def project_kernel(
    valid, pair, weight, bias, gain, shift,
    wire, mask,
    padded, by_channel, held, sems,
):
    build_mask(lax.axis_index("row"), lax.axis_index("col"), valid, mask)
    fill(padded, pair)
    gain_c, shift_c = column(gain), column(shift)
    bias_c = jnp.concatenate(columns(bias)[:4], axis=0)
    weight_t = split(weight[:, : 4 * WIDTH].T)
    by_channel[...] = order(BY_CHANNEL)

    def leave(step, side):
        lanes = pl.ds(pl.multiple_of(side * WIRE + step * STEP, STEP), STEP)
        pieces = held.at[:, lanes], wire.at[:, lanes]
        return lanes, pltpu.make_async_copy(*pieces, sems.at[2 * step + side])

    @pl.loop(0, WIRE // STEP)
    def _(step):
        sides = [], []
        for half in range(2):
            lanes = pl.ds(pl.multiple_of(half * WIRE + step * STEP, STEP), STEP)
            hat, _ = normalise(padded[lanes, :].T)
            hidden = fine(weight_t, split(hat * gain_c + shift_c)) + bias_c
            valid = mask[:, lanes]
            for side in range(2):
                value = hidden[2 * side * WIDTH : (2 * side + 1) * WIDTH]
                opened = sigmoid(hidden[(2 * side + 1) * WIDTH : (2 * side + 2) * WIDTH])
                sides[side].append((valid * opened * value).astype(BF16))
        for side in range(2):
            lanes, copy = leave(step, side)
            both = jnp.concatenate(sides[side], axis=0)
            held[:, lanes] = dot(by_channel[...], both).astype(BF16)
            copy.start()

    @pl.loop(0, WIRE // STEP)
    def _(step):
        for side in range(2):
            leave(step, side)[1].wait()


def prepare_kernel(
    mask, pair, cotangent, weight, bias, gain, shift, out_gain, out_weight,
    scale_o, saved,
    padded, padded_c, held, sems,
):
    fill(padded, pair)
    fill(padded_c, cotangent)
    gain_c, shift_c, out_gain_c = column(gain), column(shift), column(out_gain)
    bias_c = jnp.concatenate(columns(bias), axis=0)
    weight_t = split(weight[...].T)
    out_w = split(out_weight[...])

    def leave(step):
        lanes = lanes_of(step)
        return pltpu.make_async_copy(held.at[:, lanes], saved.at[:, lanes], sems.at[step])

    @pl.loop(0, STEPS)
    def _(step):
        lanes = lanes_of(step)
        hat, scale = normalise(padded[lanes, :].T)
        held[HAT:OPEN, lanes] = hat
        scale_o[:, lanes] = scale
        hidden = fine(weight_t, split(hat * gain_c + shift_c)) + bias_c
        valid = mask[:, lanes]
        for i in range(2):
            opened = sigmoid(hidden[(2 * i + 1) * WIDTH : (2 * i + 2) * WIDTH])
            factor = valid * opened
            held[2 * i * WIDTH : (2 * i + 1) * WIDTH, lanes] = factor
            held[(2 * i + 1) * WIDTH : (2 * i + 2) * WIDTH, lanes] = (
                factor * (1.0 - opened) * hidden[2 * i * WIDTH : (2 * i + 1) * WIDTH]
            )
        opened = sigmoid(hidden[4 * WIDTH :])
        held[OPEN:GIVEN, lanes] = opened
        d_result = padded_c[lanes, :].T * opened
        held[GIVEN:D_HAT, lanes] = d_result
        held[D_HAT:SAVED, lanes] = fine(out_w, split(d_result)) * out_gain_c
        leave(step).start()

    @pl.loop(0, STEPS)
    def _(step):
        leave(step).wait()


def unpack(values, out, base):
    keep = lax.broadcasted_iota(jnp.int32, (DEVICES, 128), 1) < COLS
    for i in range(HALF):
        tile, offset = divmod(i * COLS, 128)
        part = values[:, tile * 128 : tile * 128 + 256]
        if offset:
            part = pltpu.roll(part, 256 - offset, 1)
        part = jnp.where(keep, part[:, :128], 0.0).astype(BF16)
        for q in range(COL_N):
            out[pl.ds(base + i * ROW_N, ROW_N), q * 128 : (q + 1) * 128] = part[
                q * ROW_N : (q + 1) * ROW_N
            ]


def pack(values, out):
    out[...] = jnp.zeros_like(out)
    for i in range(HALF):
        tile, offset = divmod(i * COLS, 128)
        part = jnp.concatenate(
            [
                values[i * ROW_N : (i + 1) * ROW_N, q * 128 : (q + 1) * 128]
                for q in range(COL_N)
            ],
            axis=0,
        )
        part = jnp.concatenate([part, jnp.zeros_like(part)], axis=1)
        if offset:
            part = pltpu.roll(part, offset, 1)
        out[:, tile * 128 : tile * 128 + 256] += part


def mix_kernel(both_w, other_w, spread, wire, kept, left_m, right_m, packed, sems):
    own = lax.axis_index("col") % 2 * (TOTAL // 2)
    away = (TOTAL // 2) - own
    keep_left = pltpu.make_async_copy(left_m, kept.at[:LEFT_ROWS, :], sems.at[0])
    keep_right = pltpu.make_async_copy(right_m, kept.at[LEFT_ROWS:KEPT_ROWS, :], sems.at[1])
    by_col = order(BY_COL)
    unpack(dot(by_col, both_w[:, :WIRE]), left_m, 0)
    keep_left.start()
    unpack(dot(by_col, both_w[:, WIRE:]), right_m, pl.multiple_of(own, 32))
    unpack(dot(by_col, other_w[...]), right_m, pl.multiple_of(away, 32))
    keep_right.start()
    mixed = dot(left_m[...], right_m[...], LAST).astype(BF16)
    pack(dot(mixed, spread[...]), packed)
    wire[...] = move(BY_ROW, packed[...].astype(BF16)).astype(BF16)
    keep_left.wait()
    keep_right.wait()


def turn_kernel(mixed_w, saved, wire, mixed_s, d_mixed_s, d_hat, sems):
    def fetch(step):
        lanes = lanes_of(step)
        pieces = saved.at[D_HAT:SAVED, lanes], d_hat.at[:, lanes]
        return pltpu.make_async_copy(*pieces, sems.at[step])

    for step in range(STEPS):
        fetch(step).start()
    mixed_s[...] = move(BY_HALF, mixed_w[...])

    @pl.loop(0, STEPS)
    def _(step):
        rows, cols = place_of(step)
        hat, scale = normalise(mixed_s[rows, cols])
        fetch(step).wait()
        d_mixed_s[rows, cols] = normalise_back(d_hat[:, lanes_of(step)], hat, scale).astype(BF16)

    wire[...] = move(BY_CHANNEL, d_mixed_s[...]).astype(BF16)


def update_kernel(
    mixed_w, saved, weight, gain, shift, out_gain, out_shift, out_weight, out_bias,
    update, grad_out, grad_gate, d_normed,
    padded, mixed_s, held, sem,
):
    fetch = pltpu.make_async_copy(saved.at[HAT:D_HAT, :], held, sem)
    fetch.start()
    mixed_s[...] = move(BY_HALF, mixed_w[...])
    gain_c, shift_c = column(gain), column(shift)
    out_gain_c, out_shift_c, out_bias_c = column(out_gain), column(out_shift), column(out_bias)
    out_t = split(out_weight[...].T)
    gate_w = split(weight[:, 4 * WIDTH :])
    grad_out[...] = jnp.zeros_like(grad_out)
    grad_gate[...] = jnp.zeros_like(grad_gate)
    fetch.wait()

    @pl.loop(0, STEPS)
    def _(step):
        lanes = lanes_of(step)
        rows, cols = place_of(step)
        hat_m, _ = normalise(mixed_s[rows, cols])
        normed = split(hat_m * out_gain_c + out_shift_c)
        result = fine(out_t, normed) + out_bias_c
        is_open = held[OPEN - HAT : GIVEN - HAT, lanes]
        padded[lanes, :] = (is_open * result).T
        given = held[GIVEN - HAT :, lanes]
        grad_out[...] += fine(normed, split(given), LAST)
        d_gate = split(given * result * (1.0 - is_open))
        grad_gate[...] += fine(
            split(held[: OPEN - HAT, lanes] * gain_c + shift_c), d_gate, LAST
        )
        d_normed[:, lanes] = fine(gate_w, d_gate)

    drain(update, padded)


def unmix_right_kernel(
    d_w, kept, spread,
    d_mixed, own_wire, away_wire,
    d_mixed_m, terms, packed, left_m, sem,
):
    own = lax.axis_index("col") % 2 * (TOTAL // 2)
    away = (TOTAL // 2) - own
    get_left = pltpu.make_async_copy(kept.at[:LEFT_ROWS, :], left_m, sem)
    get_left.start()
    by_row = order(BY_ROW)
    unpack(move(BY_COL, d_w[...]), d_mixed_m, 0)
    d_mixed[...] = dot(d_mixed_m[...], spread[...], LAST).astype(BF16)
    get_left.wait()
    terms[...] = dot(d_mixed[...], left_m[...], ((0,), (0,)))
    pack(terms[pl.ds(pl.multiple_of(away, 32), TOTAL // 2), :], packed)
    away_wire[...] = dot(by_row, packed[...].astype(BF16)).astype(BF16)
    pack(terms[pl.ds(pl.multiple_of(own, 32), TOTAL // 2), :], packed)
    own_wire[...] = dot(by_row, packed[...].astype(BF16)).astype(BF16)


def unmix_left_kernel(d_mixed, kept, left_wire, packed, right_m, sem):
    get_right = pltpu.make_async_copy(kept.at[LEFT_ROWS:KEPT_ROWS, :], right_m, sem)
    get_right.start()
    by_row = order(BY_ROW)
    get_right.wait()
    pack(dot(d_mixed[...], right_m[...]), packed)
    left_wire[...] = dot(by_row, packed[...].astype(BF16)).astype(BF16)


def d_hidden_of(d_left_s, d_right_s, factors, step):
    rows, cols = place_of(step)
    lanes = lanes_of(step)
    parts = []
    for i, ref in enumerate((d_left_s, d_right_s)):
        given = ref[rows, cols]
        for j in range(2):
            start = (2 * i + j) * WIDTH
            parts.append(given * factors[start : start + WIDTH, lanes])
    return split(jnp.concatenate(parts, axis=0))


def fetch_saved(saved, held, sems, step):
    lanes = lanes_of(step)
    return pltpu.make_async_copy(saved.at[:OPEN, lanes], held.at[:, lanes], sems.at[step])


def weight_kernel(
    both_w, saved, gain, shift, grad_gate, grad_out,
    grads,
    d_left_s, d_right_s, total, held, sems,
):
    for step in range(STEPS):
        fetch_saved(saved, held, sems, step).start()
    by_half = order(BY_HALF)
    d_left_s[...] = dot(by_half, both_w[:, :WIRE])
    d_right_s[...] = dot(by_half, both_w[:, WIRE:])
    gain_c, shift_c = column(gain), column(shift)
    total[...] = jnp.zeros_like(total)

    @pl.loop(0, STEPS)
    def _(step):
        fetch_saved(saved, held, sems, step).wait()
        d_hidden = d_hidden_of(d_left_s, d_right_s, held, step)
        normed = split(held[HAT:OPEN, lanes_of(step)] * gain_c + shift_c)
        total[...] += fine(normed, d_hidden, LAST)

    grads[:WIDTH, :] = total[:, : 3 * WIDTH]
    grads[WIDTH:, :WIDTH] = total[:, 3 * WIDTH :]
    grads[WIDTH:, WIDTH : 2 * WIDTH] = grad_gate[...]
    grads[WIDTH:, 2 * WIDTH :] = grad_out[...]


def pair_kernel(
    both_w, saved, scale, d_normed, weight, gain,
    grad_pair,
    d_left_s, d_right_s, padded, held, sems,
):
    for step in range(STEPS):
        fetch_saved(saved, held, sems, step).start()
    by_half = order(BY_HALF)
    d_left_s[...] = dot(by_half, both_w[:, :WIRE])
    d_right_s[...] = dot(by_half, both_w[:, WIRE:])
    gain_c = column(gain)
    weight_s = split(weight[:, : 4 * WIDTH])

    @pl.loop(0, STEPS)
    def _(step):
        fetch_saved(saved, held, sems, step).wait()
        lanes = lanes_of(step)
        d_hidden = d_hidden_of(d_left_s, d_right_s, held, step)
        d_hat = (fine(weight_s, d_hidden) + d_normed[:, lanes]) * gain_c
        padded[lanes, :] = normalise_back(d_hat, held[HAT:OPEN, lanes], scale[:, lanes]).T

    drain(grad_pair, padded)


def join_kernel(own, other, grad_proj, grad_out):
    first = lax.axis_index("col") % 2 == 0
    own, other = own[...].astype(F32), other[...].astype(F32)
    upper, lower = jnp.where(first, own, other), jnp.where(first, other, own)
    grad_proj[:, : 3 * WIDTH] = upper
    grad_proj[:, 3 * WIDTH :] = lower[:, : 2 * WIDTH]
    grad_out[...] = lower[:, 2 * WIDTH :]


class Raw:
    def __init__(self, value):
        self.value = value


def call(kernel, outs, scratch, *args, smem=0, work=2e9, room=48):
    operands = [a.value if isinstance(a, Raw) else a for a in args]
    results = [jax.ShapeDtypeStruct(*(o.value if isinstance(o, Raw) else o)) for o in outs]

    def spec(value, raw):
        if raw:
            return pl.BlockSpec(memory_space=pl.ANY)
        return pl.BlockSpec(value.shape, lambda i: (0,) * len(value.shape))

    specs = [spec(v, isinstance(w, Raw)) for v, w in zip([*operands, *results], [*args, *outs])]
    specs[:smem] = [pl.BlockSpec(memory_space=pltpu.SMEM)] * smem
    return pl.pallas_call(
        kernel,
        grid=(1,),
        out_shape=results,
        in_specs=specs[: len(args)],
        out_specs=specs[len(args) :],
        scratch_shapes=[pltpu.VMEM(*s) if isinstance(s, tuple) else s for s in scratch],
        compiler_params=pltpu.CompilerParams(vmem_limit_bytes=room * 2**20),
        cost_estimate=pl.CostEstimate(flops=int(work), bytes_accessed=4 * 2**20, transcendentals=0),
    )(*operands)


def spin(step, count, inner):
    size = 32 if inner != 2 else 8
    return [
        (i, i - (i // inner % count) * inner + ((i // inner + step) % count) * inner)
        for i in range(size)
    ]


LINES = [
    [(y * 8 + high * 4 + x) * COL_N + low * 2 + core for high in range(2) for low in range(4)]
    for y in range(4)
    for x in range(4)
    for core in range(2)
]


def meet(value, axis, count, inner):
    others = [lax.ppermute(value, axis, spin(k, count, inner)) for k in range(1, count)]
    if count == 2:
        return value + others[0]
    one, two, three = others
    return (value + two) + (one + three)


def sum_over_devices(grads, row, col, beside):
    core, x = col % 2, row % 4
    pick = lambda a, i: lax.dynamic_index_in_dim(a, i, 0, keepdims=False)
    pairs = grads.reshape(2, WIDTH, 3 * WIDTH)
    taken = lax.ppermute(pick(pairs, 1 - core), "col", SWAP)
    total = pick(pairs, core) + taken
    total = total.reshape(4, WIDTH // 4, 3 * WIDTH)
    taken = [
        lax.ppermute(pick(total, (x + k) % 4), "row", spin(k, 4, 1)) for k in (1, 2, 3)
    ]
    total = (pick(total, x) + taken[0]) + (taken[1] + taken[2])
    total = meet(total, "row", 4, 8)
    total = jnp.broadcast_to(total.astype(BF16)[None], (8,) + total.shape)
    total = lax.all_to_all(total, BOTH, 0, 0, axis_index_groups=LINES, tiled=True)
    total = jnp.sum(total.astype(F32), axis=0).astype(BF16)
    total, beside = lax.optimization_barrier((total, beside))
    parts = jnp.zeros((4, WIDTH // 4, 3 * WIDTH), BF16)
    parts = lax.dynamic_update_index_in_dim(parts, total, x, 0)
    for k in (1, 2, 3):
        taken = lax.ppermute(total, "row", spin(k, 4, 1))
        parts = lax.dynamic_update_index_in_dim(parts, taken, (x + 4 - k) % 4, 0)
    parts = parts.reshape(WIDTH, 3 * WIDTH)
    other = lax.ppermute(parts, "col", SWAP)
    return parts, other, beside


def exchange(chunks):
    return lax.all_to_all(chunks, BOTH, 0, 0, tiled=True)


def shards(
    pair,
    cotangent,
    residue_mask,
    ln_gain,
    ln_bias,
    proj_weight,
    proj_bias,
    norm_gain,
    norm_bias,
    out_weight,
    out_bias,
):
    spread = spread_table()
    shape = pair.shape
    places = ROWS * COLS
    row, col = lax.axis_index("row"), lax.axis_index("col")
    pair = pair.reshape(places, WIDTH)
    cotangent = cotangent.reshape(places, WIDTH)
    line = lambda v: v.reshape(-1, WIDTH)
    gain, shift, bias = line(ln_gain), line(ln_bias), line(proj_bias)
    out_gain, out_shift, out_bias = line(norm_gain), line(norm_bias), line(out_bias)
    whole = ((LANES, WIDTH), F32)
    turned = ((WIDTH, LANES), F32)
    square = ((WIDTH, WIDTH), F32)
    halves = lambda kind: ((DEVICES, WIRE), kind)

    dma = pltpu.SemaphoreType.DMA
    wire, mask = call(
        project_kernel,
        [Raw(((DEVICES, LANES), BF16)), ((1, LANES), F32)],
        [whole, ((DEVICES, DEVICES), BF16), ((DEVICES, LANES), BF16), dma((STEPS,))],
        residue_mask, pair, proj_weight, bias, gain, shift,
        smem=1,
        room=63,
    )
    got = exchange(wire.reshape(DEVICES, 2, WIRE)).reshape(DEVICES, LANES)
    scale, saved = call(
        prepare_kernel,
        [((1, LANES), F32), Raw(((SAVED, LANES), F32))],
        [whole, whole, ((SAVED, LANES), F32), dma((STEPS,))],
        mask, pair, cotangent, proj_weight, bias, gain, shift, out_gain, out_weight,
        work=1e10,
    )
    other_w = lax.ppermute(got[:, WIRE:], "col", SWAP)
    left_s, right_s = ((LEFT_ROWS, COL_N * 128), BF16), ((TOTAL, COL_N * 128), BF16)
    wire, kept = call(
        mix_kernel,
        [halves(BF16), Raw(((KEPT, COL_N * 128), BF16))],
        [left_s, right_s, halves(F32), dma((2,))],
        got, other_w, spread,
    )
    mixed_w = exchange(wire.reshape(DEVICES, 2, WIRE // 2)).reshape(DEVICES, WIRE)
    (wire,) = call(
        turn_kernel,
        [halves(BF16)],
        [halves(F32), halves(BF16), turned, dma((STEPS,))],
        mixed_w, Raw(saved),
    )
    got = exchange(wire.reshape(DEVICES, 2, WIRE // 2)).reshape(DEVICES, WIRE)
    update, grad_out, grad_gate, d_normed = call(
        update_kernel,
        [((places, WIDTH), F32), square, square, turned],
        [whole, halves(F32), ((D_HAT - HAT, LANES), F32), dma],
        mixed_w, Raw(saved), proj_weight, gain, shift, out_gain, out_shift, out_weight, out_bias,
        work=8e9,
    )
    d_mixed, own_wire, away_wire = call(
        unmix_right_kernel,
        [((LEFT_ROWS, TOTAL), BF16), halves(BF16), halves(BF16)],
        [left_s, ((TOTAL, COL_N * 128), F32), halves(F32), left_s, dma],
        got, Raw(kept), spread,
    )
    other_wire = lax.ppermute(away_wire, "col", SWAP)
    (left_wire,) = call(
        unmix_left_kernel,
        [halves(BF16)],
        [halves(F32), right_s, dma],
        d_mixed, Raw(kept),
    )
    right_wire = (own_wire.astype(F32) + other_wire.astype(F32)).astype(BF16)
    got = exchange(jnp.stack([left_wire, right_wire], axis=1)).reshape(DEVICES, LANES)
    held = ((OPEN, LANES), F32)
    (grads,) = call(
        weight_kernel,
        [((DEVICES, 3 * WIDTH), F32)],
        [halves(F32), halves(F32), ((WIDTH, 4 * WIDTH), F32), held, dma((STEPS,))],
        got, Raw(saved), gain, shift, grad_gate, grad_out,
    )
    (grad_pair,) = call(
        pair_kernel,
        [((places, WIDTH), F32)],
        [halves(F32), halves(F32), whole, held, dma((STEPS,))],
        got, Raw(saved), scale, d_normed, proj_weight, gain,
        work=8e9,
    )
    own, other, grad_pair = sum_over_devices(grads, row, col, grad_pair)
    grad_proj, grad_out = call(
        join_kernel, [((WIDTH, 5 * WIDTH), F32), square], [], own, other, work=1e8
    )
    return update.reshape(shape), grad_pair.reshape(shape), grad_proj, grad_out


def solution(mesh):
    in_specs = (P("row", "col", None), P("row", "col", None)) + (P(),) * 9
    out_specs = (P("row", "col", None), P("row", "col", None), P(), P())
    return jax.shard_map(shards, mesh=mesh, in_specs=in_specs, out_specs=out_specs, check_vma=False)
```
